32 devices in a mesh: groups: 2 (over y), ep: 4 (over z), tp: 4 (over x, core).
Axes of the slice: x: 2, y: 2, z: 4, core: 2. Of those that a mesh axis runs over, the one named last changes fastest.
Arguments:
- queries: bfloat16 [256, 8192], P(('groups', 'ep'), 'tp'), parts along dimension 0, may hold values from -4.5 to 4.5
- cached_key_table: bfloat16 [256, 128, 512], P(('groups', 'ep'), None, 'tp'), parts along dimension 0, may hold values from -4.5 to 4.5
- cached_value_table: bfloat16 [256, 128, 512], P(('groups', 'ep'), None, 'tp'), parts along dimension 0, may hold values from -10 to 10
- fresh_token_keys: bfloat16 [256, 512], P(('groups', 'ep'), 'tp'), parts along dimension 0, may hold values from -4.5 to 4.5
- fresh_token_values: bfloat16 [256, 512], P(('groups', 'ep'), 'tp'), parts along dimension 0, may hold values from -10 to 10
- cache_len: int32 [256], P(('groups', 'ep')), parts along dimension 0, may hold values from 1 to 128, as said below
- out_proj: bfloat16 [8192, 4096], P('tp', 'ep'), may hold values from -0.0625 to 0.0625
- residual: bfloat16 [256, 4096], P(('groups', 'ep'), 'tp'), parts along dimension 0, may hold values from -10.5 to 10.5
- norm_gain: bfloat16 [4096], replicated, may hold values from 0.099609375 to 1.8984375
- routes: int32 [256, 8], P(('groups', 'ep')), parts along dimension 0, may hold values from 0 to 7, as said below
- gate_weights: float32 [256, 8], P(('groups', 'ep')), parts along dimension 0, may hold values from 0.05 to 0.4
- gate_proj: bfloat16 [8, 768, 4096], P('ep', 'tp'), may hold values from -0.09375 to 0.09375
- up_proj: bfloat16 [8, 768, 4096], P('ep', 'tp'), may hold values from -0.09375 to 0.09375
- down_proj: bfloat16 [8, 768, 4096], P('ep', 'tp'), may hold values from -0.21875 to 0.21875
Outputs:
- layer_out: bfloat16 [256, 4096], P(('groups', 'ep'), 'tp'), parts along dimension 0
The draws below stay inside these ranges and needn't reach their ends.
There are 2 independent parts, one for each index of `groups`. The reference program is written for one: setup_inputs(seed, part) draws one part's arguments, and reference() takes and returns one part's arrays. A program takes and returns all parts, laid end to end along the dimension named above; an argument that names none is the same for every part. Nothing has to cross between parts.
Inputs may be any that keep to these rules, and one draw needn't show every extreme that they name: Row r uses the cache positions below cache_len[r]; some row uses all 128. `routes`: each row names 8 different experts. Among the rows of one ep index no expert is named more than 32 times, and one expert, the same for every ep index, is named exactly 32 times by the rows of each index.
All inputs are finite; a program needn't handle non-finite values.
Results may differ from the reference program's by a relative error of at most 0.008.
Values may be sent and summed in bfloat16 or wider, within the bound.
A program may use at most 128 MiB of HBM per device.

```python
import math
import jax
import jax.numpy as jnp
from jax import lax

D = 4096
QUERY_HEADS = 64
KEY_VALUE_HEADS = 4
HEAD_DIM = 128
FF = 768
TOP = 8
ROWS_DEV = 32
CACHE_SLOTS = 128
EXPERTS = 8
DECODE_ROWS = 128
CAP = 32
N_EP = 4


def draw_queries(key, part):
    key = jax.random.fold_in(key, 1)
    values_float = jnp.clip(jax.random.normal(key, (DECODE_ROWS, QUERY_HEADS * HEAD_DIM), jnp.float32), -4.0, 4.0)
    return values_float.astype(jnp.bfloat16)


def draw_cached_key_table(key, part):
    key = jax.random.fold_in(key, 2)
    values_float = jnp.clip(jax.random.normal(key, (DECODE_ROWS, CACHE_SLOTS, KEY_VALUE_HEADS * HEAD_DIM), jnp.float32), -4.0, 4.0)
    return values_float.astype(jnp.bfloat16)


def draw_fresh_token_keys(key, part):
    key = jax.random.fold_in(key, 3)
    values_float = jnp.clip(jax.random.normal(key, (DECODE_ROWS, KEY_VALUE_HEADS * HEAD_DIM), jnp.float32), -4.0, 4.0)
    return values_float.astype(jnp.bfloat16)


def draw_cache_len(key, part):
    key = jax.random.fold_in(key, 4)
    sub_keys = jax.random.split(key, 2)
    lengths = jax.random.randint(sub_keys[0], (DECODE_ROWS,), 1, CACHE_SLOTS + 1)
    full_row = jax.random.randint(sub_keys[1], (), 0, DECODE_ROWS)
    return lengths.at[full_row].set(CACHE_SLOTS).astype(jnp.int32)


def draw_routes(key, part):
    key = jax.random.fold_in(key, 5)
    pick_count = ROWS_DEV * TOP
    mean_load = pick_count // EXPERTS
    sub_keys = jax.random.split(key, 2)
    hottest = jax.random.randint(sub_keys[0], (), 0, EXPERTS)
    rank_ids = jnp.arange(EXPERTS)

    def one_block(block_seed):
        seeds = jax.random.split(block_seed, 5)
        if 2 * mean_load <= ROWS_DEV:
            paired = jax.random.randint(seeds[0], (), 1, EXPERTS // 4 + 1)
            shifted = jax.random.randint(seeds[1], (), 0, (EXPERTS - 2 * paired) // 2 + 1)
        else:
            paired = jnp.int32(0)
            shifted = jnp.int32(0)
        scores = jnp.where(rank_ids == hottest, -1, jax.random.permutation(seeds[2], EXPERTS))
        expert_order = jnp.argsort(scores)
        counts = jnp.where(rank_ids < paired, 2 * mean_load, jnp.where(rank_ids < 2 * paired, 0, jnp.where(rank_ids < 2 * paired + shifted, mean_load + 1, jnp.where(rank_ids < 2 * paired + 2 * shifted, mean_load - 1, mean_load))))
        run_ends = jnp.cumsum(counts)
        positions = jnp.arange(pick_count)
        run_index = jnp.sum(run_ends[None, :] <= positions[:, None], axis=1)
        listed = expert_order[run_index]
        listed = jnp.roll(listed, jax.random.randint(seeds[3], (), 0, pick_count))
        block_table = listed.reshape(TOP, ROWS_DEV).T
        return block_table[jax.random.permutation(seeds[4], ROWS_DEV)]
    blocks = jax.vmap(one_block)(jax.random.split(sub_keys[1], DECODE_ROWS // ROWS_DEV))
    return blocks.reshape(DECODE_ROWS, TOP).astype(jnp.int32)


def draw_residual(key, part):
    key = jax.random.fold_in(key, 7)
    sub_keys = jax.random.split(key, 3)
    col_ramp = 1.0 + 2.0 * jnp.arange(D, dtype=jnp.float32) / (D - 1)
    col_scale = jnp.exp(jax.random.uniform(sub_keys[1], (D,), jnp.float32, jnp.log(0.5), jnp.log(1.5)))
    row_scale = jnp.exp(jax.random.uniform(sub_keys[2], (DECODE_ROWS, 1), jnp.float32, jnp.log(0.2), jnp.log(2.0)))
    normal_part = jnp.clip(jax.random.normal(sub_keys[0], (DECODE_ROWS, D), jnp.float32), -3.0, 3.0)
    return (0.25 * row_scale * col_ramp * col_scale * normal_part).astype(jnp.bfloat16)


def block_levels(rng, shape, cuts, smallest, high):
    def one(dim, parts):
        steps = jax.random.uniform(jax.random.fold_in(jax.random.fold_in(rng, 6), dim), (parts,), jnp.float32, smallest / len(cuts), high / len(cuts))
        return jnp.repeat(jnp.exp(steps), shape[dim] // parts).reshape((-1,) + (1,) * (len(shape) - dim - 1))

    factor_of = one(*cuts[0])
    for cut in cuts[1:]:
        factor_of = factor_of * one(*cut)
    return factor_of


def bell_draw(stream_key, extent, width, reach, pieces=(), kind=jnp.bfloat16):
    values = jax.random.normal(stream_key, extent, jnp.float32) * width
    if len(pieces) > 0:
        values = block_levels(stream_key, extent, pieces, -0.22, 0.18) * values
    return jnp.clip(values, min=-reach, max=reach).astype(kind)


def setup_inputs(seed: int = 0, part: int = 0) -> dict:
    streams_of = jax.random.split(jax.random.key(seed), 15)
    own_keys = jax.random.split(jax.random.fold_in(streams_of[14], part), 15)
    queries = draw_queries(jax.random.fold_in(jax.random.fold_in(streams_of[14], part), 71), part)
    cached_key_table = draw_cached_key_table(jax.random.fold_in(jax.random.fold_in(streams_of[14], part), 71), part)
    cached_value_table = bell_draw(own_keys[2], (DECODE_ROWS, CACHE_SLOTS, KEY_VALUE_HEADS * HEAD_DIM), 2.5, 10.0, ((0, 4), (2, 4)))
    fresh_token_keys = draw_fresh_token_keys(jax.random.fold_in(jax.random.fold_in(streams_of[14], part), 71), part)
    fresh_token_values = bell_draw(own_keys[4], (DECODE_ROWS, KEY_VALUE_HEADS * HEAD_DIM), 2.5, 10.0, ((0, 4), (1, 4)))
    cache_len = draw_cache_len(jax.random.fold_in(jax.random.fold_in(streams_of[14], part), 71), part)
    out_proj = bell_draw(streams_of[6], (QUERY_HEADS * HEAD_DIM, D), (QUERY_HEADS * HEAD_DIM) ** -0.5, 0.0625, ((0, 4), (1, 4)))
    residual = draw_residual(jax.random.fold_in(jax.random.fold_in(streams_of[14], part), 71), part)
    norm_gain = jnp.clip(1.0 + 0.18 * jax.random.normal(streams_of[8], (D,), jnp.float32), 0.099609375, 1.8984375).astype(jnp.bfloat16)
    routes = draw_routes(jax.random.fold_in(jax.random.fold_in(streams_of[14], part), 71), part)
    gate_weights = jnp.clip(jnp.exp(math.log(0.4) - 2.0794415 * jax.random.uniform(own_keys[10], (DECODE_ROWS, TOP), jnp.float32) ** block_levels(own_keys[10], (DECODE_ROWS, TOP), ((0, 4),), -0.2, 0.2)), 0.05, 0.4)
    gate_proj = bell_draw(streams_of[11], (EXPERTS, FF, D), D ** -0.5, 0.09375, ((0, 4), (1, 4)))
    up_proj = bell_draw(streams_of[12], (EXPERTS, FF, D), D ** -0.5, 0.09375, ((0, 4), (1, 4)))
    down_proj = bell_draw(streams_of[13], (EXPERTS, FF, D), FF ** -0.5, 0.21875, ((0, 4), (1, 4)))
    return dict(queries=queries, cached_key_table=cached_key_table, cached_value_table=cached_value_table, fresh_token_keys=fresh_token_keys, fresh_token_values=fresh_token_values, cache_len=cache_len, out_proj=out_proj, residual=residual, norm_gain=norm_gain, routes=routes, gate_weights=gate_weights, gate_proj=gate_proj, up_proj=up_proj, down_proj=down_proj)


def attention_all(queries, cached_key_table, cached_value_table, fresh_token_keys, fresh_token_values, cache_len):
    query_group_width = QUERY_HEADS // KEY_VALUE_HEADS
    every_row_index = queries.shape[0]
    query_float = queries.astype(jnp.float32).reshape(every_row_index, KEY_VALUE_HEADS, query_group_width, HEAD_DIM)
    keys_float = cached_key_table.astype(jnp.float32).reshape(every_row_index, CACHE_SLOTS, KEY_VALUE_HEADS, HEAD_DIM)
    values_float = cached_value_table.astype(jnp.float32).reshape(every_row_index, CACHE_SLOTS, KEY_VALUE_HEADS, HEAD_DIM)
    fresh_key_float = fresh_token_keys.astype(jnp.float32).reshape(every_row_index, KEY_VALUE_HEADS, HEAD_DIM)
    fresh_value_float = fresh_token_values.astype(jnp.float32).reshape(every_row_index, KEY_VALUE_HEADS, HEAD_DIM)
    score_scale = 1.0 / math.sqrt(HEAD_DIM)
    scores = jnp.einsum('rkgd,rjkd->rkgj', query_float, keys_float) * score_scale
    own_score = jnp.einsum('rkgd,rkd->rkg', query_float, fresh_key_float) * score_scale
    usable = jnp.arange(CACHE_SLOTS, dtype=jnp.int32)[None, :] < cache_len[:, None]
    scores = jnp.where(usable[:, None, None, :], scores, -jnp.inf)
    highest = jnp.maximum(lax.optimization_barrier(jnp.max(scores, axis=-1)), own_score)
    exp_scores = jnp.exp(scores - highest[..., None])
    own_exp = jnp.exp(own_score - highest)
    denominator = lax.optimization_barrier(jnp.sum(exp_scores, axis=-1)) + own_exp
    attn_probs = lax.optimization_barrier((exp_scores / denominator[..., None]).astype(jnp.bfloat16))
    own_prob = lax.optimization_barrier((own_exp / denominator).astype(jnp.bfloat16))
    attended = jnp.einsum('rkgj,rjkd->rkgd', attn_probs.astype(jnp.float32), values_float)
    attended = attended + own_prob.astype(jnp.float32)[..., None] * fresh_value_float[:, :, None, :]
    return attended.reshape(every_row_index, QUERY_HEADS * HEAD_DIM).astype(jnp.bfloat16)

def reference(queries, cached_key_table, cached_value_table, fresh_token_keys, fresh_token_values, cache_len, out_proj, residual, norm_gain, routes, gate_weights, gate_proj, up_proj, down_proj):
    attended = attention_all(queries, cached_key_table, cached_value_table, fresh_token_keys, fresh_token_values, cache_len)
    hidden = residual.astype(jnp.float32) + jnp.dot(attended, out_proj, preferred_element_type=jnp.float32)
    mean_square = lax.optimization_barrier(jnp.mean(hidden * hidden, axis=-1, keepdims=True))
    normed = (hidden * lax.rsqrt(mean_square + 1e-06) * norm_gain.astype(jnp.float32)).astype(jnp.bfloat16)
    every_row_index = normed.shape[0]
    pair_count = every_row_index * TOP
    flat_routes = routes.reshape(-1).astype(jnp.int32)
    capacity = N_EP * CAP

    def run_expert(expert):
        chosen = jnp.nonzero(flat_routes == expert, size=capacity, fill_value=pair_count)[0].astype(jnp.int32)
        source_rows = jnp.minimum(chosen // TOP, every_row_index - 1).astype(jnp.int32)
        inputs = normed[source_rows]
        gate_part = jnp.dot(inputs, gate_proj[expert].T, preferred_element_type=jnp.float32)
        up_part = jnp.dot(inputs, up_proj[expert].T, preferred_element_type=jnp.float32)
        activated = (jax.nn.silu(gate_part) * up_part).astype(jnp.bfloat16)
        produced = jnp.dot(activated, down_proj[expert], preferred_element_type=jnp.float32)
        return (produced, chosen)
    produced, chosen = lax.map(run_expert, jnp.arange(EXPERTS, dtype=jnp.int32))
    pair_out = jnp.zeros((pair_count + 1, D), jnp.float32).at[chosen.reshape(-1)].set(produced.reshape(-1, D))
    pair_out = pair_out[:pair_count].reshape(every_row_index, TOP, D)
    mixture = lax.optimization_barrier(jnp.sum(gate_weights.astype(jnp.float32)[:, :, None] * pair_out, axis=1))
    return (hidden + mixture).astype(jnp.bfloat16)
```

```python
import functools
import math

import jax
import jax.numpy as jnp
from jax import lax
from jax.experimental import pallas as pl
from jax.experimental.pallas import tpu as pltpu
from jax.sharding import PartitionSpec as P

HEAD_DIM = 128
TOP = 8


def attend_local(
    queries, cached_key_table, cached_value_table, fresh_token_keys, fresh_token_values, cache_len
):
    rows_here = queries.shape[0]
    kv_heads = cached_key_table.shape[2] // HEAD_DIM
    query_group_width = queries.shape[1] // HEAD_DIM // kv_heads
    cache_size = cached_key_table.shape[1]
    query_block = queries.reshape(rows_here, kv_heads, query_group_width, HEAD_DIM)
    key_block = cached_key_table.reshape(rows_here, cache_size, kv_heads, HEAD_DIM)
    value_block = cached_value_table.reshape(rows_here, cache_size, kv_heads, HEAD_DIM)
    newkey_block = fresh_token_keys.reshape(rows_here, kv_heads, HEAD_DIM)
    newval_block = fresh_token_values.reshape(rows_here, kv_heads, HEAD_DIM)
    score_scale = 1.0 / math.sqrt(HEAD_DIM)
    scores = (
        jnp.einsum("rkgd,rjkd->rkgj", query_block, key_block, preferred_element_type=jnp.float32)
        * score_scale
    )
    own_score = (
        jnp.einsum("rkgd,rkd->rkg", query_block, newkey_block, preferred_element_type=jnp.float32)
        * score_scale
    )
    usable = jnp.arange(cache_size, dtype=jnp.int32)[None, :] < cache_len[:, None]
    scores = jnp.where(usable[:, None, None, :], scores, -jnp.inf)
    highest = jnp.maximum(jnp.max(scores, axis=-1), own_score)
    exp_scores = jnp.exp(scores - highest[..., None])
    own_exp = jnp.exp(own_score - highest)
    denominator = jnp.sum(exp_scores, axis=-1) + own_exp
    attn_probs = (exp_scores / denominator[..., None]).astype(jnp.bfloat16)
    own_prob = (own_exp / denominator).astype(jnp.bfloat16)
    attended = jnp.einsum(
        "rkgj,rjkd->rkgd", attn_probs, value_block, preferred_element_type=jnp.float32
    )
    attended = (
        attended
        + own_prob.astype(jnp.float32)[..., None] * newval_block.astype(jnp.float32)[:, :, None, :]
    )
    return attended.reshape(rows_here, -1).astype(jnp.bfloat16)


def per_device(
    queries,
    cached_key_table,
    cached_value_table,
    fresh_token_keys,
    fresh_token_values,
    cache_len,
    out_proj,
    residual,
    norm_gain,
    routes,
    gate_weights,
    gate_proj,
    up_proj,
    down_proj,
):
    attended = attend_local(
        queries,
        cached_key_table,
        cached_value_table,
        fresh_token_keys,
        fresh_token_values,
        cache_len,
    )
    partial_all = jnp.dot(
        lax.all_gather(attended, "ep", axis=0, tiled=True),
        out_proj,
        preferred_element_type=jnp.float32,
    )
    partial_rows = lax.all_to_all(partial_all, "ep", split_axis=0, concat_axis=1, tiled=True)
    ep_count = lax.axis_size("ep")
    tp_index = lax.axis_index("tp")
    rows_here = residual.shape[0]
    col_width = residual.shape[1]
    local_experts = gate_proj.shape[0]
    expert_count = local_experts * ep_count
    capacity = min(rows_here, 2 * rows_here * TOP // expert_count)
    flat_routes = routes.reshape(-1)
    pair_count = flat_routes.shape[0]
    member = (flat_routes[:, None] == jnp.arange(expert_count, dtype=jnp.int32)[None, :]).astype(
        jnp.int32
    )
    earlier = jnp.cumsum(member, axis=0) - member
    position = jnp.sum(earlier * member, axis=1)
    target = flat_routes * capacity + position
    slot_match = (
        jnp.arange(expert_count * capacity, dtype=jnp.int32)[:, None] == target[None, :]
    ).astype(jnp.int32)
    occupied = jnp.sum(slot_match, axis=1)
    source_row = jnp.sum(
        slot_match * (jnp.arange(pair_count, dtype=jnp.int32) // TOP)[None, :], axis=1
    )
    gain_full = norm_gain.astype(jnp.float32)
    own_cols = lax.dynamic_slice_in_dim(
        partial_rows, tp_index * col_width, col_width, 1
    ) + residual.astype(jnp.float32)
    with_residual = lax.dynamic_update_slice_in_dim(partial_rows, own_cols, tp_index * col_width, 1)
    hidden_full = lax.psum(with_residual, "tp")
    mean_square = jnp.mean(hidden_full * hidden_full, axis=-1, keepdims=True)
    normed = (hidden_full * lax.rsqrt(mean_square + 1e-06) * gain_full).astype(jnp.bfloat16)
    hidden = lax.dynamic_slice_in_dim(hidden_full, tp_index * col_width, col_width, 1)
    picked = jnp.where(occupied[:, None] > 0, normed[source_row], jnp.zeros((), normed.dtype))
    arrived = lax.all_to_all(
        picked.reshape(ep_count, local_experts, capacity, normed.shape[1]),
        "ep",
        split_axis=0,
        concat_axis=0,
        tiled=True,
    )
    gate_part = jnp.einsum("aesd,efd->aesf", arrived, gate_proj, preferred_element_type=jnp.float32)
    up_part = jnp.einsum("aesd,efd->aesf", arrived, up_proj, preferred_element_type=jnp.float32)
    activated = (jax.nn.silu(gate_part) * up_part).astype(jnp.bfloat16)
    partial_out = jnp.einsum(
        "aesf,efd->aesd", activated, down_proj, preferred_element_type=jnp.float32
    )
    reduced = lax.psum_scatter(
        partial_out.astype(jnp.bfloat16), "tp", scatter_dimension=3, tiled=True
    ).astype(jnp.float32)
    returned = lax.all_to_all(
        reduced.astype(jnp.bfloat16), "ep", split_axis=0, concat_axis=0, tiled=True
    ).astype(reduced.dtype)
    flat_back = returned.reshape(expert_count * capacity, col_width)
    pair_out = flat_back[target].reshape(rows_here, TOP, col_width)
    mixture = jnp.sum(gate_weights[:, :, None] * pair_out, axis=1)
    return (hidden + mixture).astype(jnp.bfloat16)


MESH = pl.DeviceIdType.MESH
N = 4
BF = jnp.bfloat16
F32 = jnp.float32


def dot_nt(a, b):
    return lax.dot_general(a, b, (((1,), (1,)), ((), ())), preferred_element_type=F32)


def layer_kernel(
    len_ref, q_ref, ck_hbm, cv_hbm, nk_ref, nv_ref, wo_hbm, res_ref, gain_ref, routes_ref, gw_ref,
    g_hbm, u_hbm, d_hbm, out_ref,
    ck, cv, wo, gw, uw, dw, qs, ao, nk32, nv32, gain32, rgain, att, res_all, w_all,
    part, c1s, c1r, hg, ga, ua, ss, act, ecs, ecr, p1, p3, xs, xr, zs, zr,
    load_sem, res_s, res_r, w_s, w_r, a_s, a_f, a_r, c1_s, c1_rs, cz_s, cz_f, cz_r, cx_s, cx_r,
    cc_s, cc_r, ec_s, ec_r, ex_s, ex_r, ez_s, ez_r,
):
    rows, heads = q_ref.shape[0], q_ref.shape[1] // HEAD_DIM
    slots = ck.shape[1]
    width = res_ref.shape[1]
    quarter = width // N
    half_rows = rows // 2
    z = lax.axis_index("ep")
    t = lax.axis_index("tp")
    core, xpos = lax.rem(t, 2), t // 2
    t_core = 2 * xpos + (1 - core)
    t_x = 2 * (1 - xpos) + core
    t_diag = 2 * (1 - xpos) + (1 - core)
    order = [
        z,
        jnp.where(z == 0, 1, z - 1),
        jnp.where(z == 0, 2, jnp.where(z == N - 1, 1, z + 1)),
        jnp.where(z <= 1, 3, 0),
    ]
    always = z >= 0
    sends = []

    def load(i, src, dst):
        copy = pltpu.make_async_copy(src, dst, load_sem.at[i])
        copy.start()
        return copy

    def send(src, dst, s_sem, r_sem, where, cond=None):
        copy = pltpu.make_async_remote_copy(
            src_ref=src, dst_ref=dst, send_sem=s_sem, recv_sem=r_sem, device_id=where,
            device_id_type=MESH,
        )
        if cond is None:
            copy.start()
        else:
            pl.when(cond)(lambda: copy.start())
        sends.append((copy, cond))

    def arrived(dst, s_sem, r_sem):
        pltpu.make_async_remote_copy(
            src_ref=dst, dst_ref=dst, send_sem=s_sem, recv_sem=r_sem, device_id={"ep": z},
            device_id_type=MESH,
        ).wait_recv()

    loads = []
    for h in range(2):
        piece = pl.ds(h * half_rows, half_rows)
        loads.append(load(2 * h, ck_hbm.at[piece], ck.at[piece]))
        loads.append(load(2 * h + 1, cv_hbm.at[piece], cv.at[piece]))
    load_wo = load(4, wo_hbm, wo)

    barrier = pltpu.get_barrier_semaphore()
    for k in range(1, N):
        pl.semaphore_signal(barrier, inc=1, device_id={"ep": lax.rem(z + k, N)}, device_id_type=MESH)
        pl.semaphore_signal(barrier, inc=1, device_id={"tp": lax.rem(t + k, N)}, device_id_type=MESH)

    lane = lax.broadcasted_iota(jnp.int32, (rows, 128), 1)
    dense = jnp.zeros((rows, 128), F32)
    for k in range(TOP):
        dense = dense + jnp.where(lane == routes_ref[:, k : k + 1], gw_ref[:, k : k + 1], 0.0)
    w_all[z] = dense
    for h in range(heads):
        qs[pl.ds(h, rows, stride=heads), :] = q_ref[:, h * HEAD_DIM : (h + 1) * HEAD_DIM].astype(F32)
    nk32[...] = nk_ref[...].astype(F32)
    nv32[...] = nv_ref[...].astype(F32)
    gain32[...] = gain_ref[...].astype(F32)
    rgain[...] = 1.0 / gain32[...]
    ga[...] = jnp.zeros_like(ga)
    ua[...] = jnp.zeros_like(ua)
    ss[...] = jnp.zeros_like(ss)

    pl.semaphore_wait(barrier, 2 * (N - 1))

    send(res_ref, res_all.at[z], res_s.at[0], res_r.at[z], {"ep": t}, z != t)
    for k in range(1, N):
        send(w_all.at[z], w_all.at[z], w_s.at[k], w_r.at[z], {"ep": lax.rem(z + k, N)})

    score_scale = 1.0 / math.sqrt(HEAD_DIM)
    position = lax.broadcasted_iota(jnp.int32, (heads, slots), 1)
    group = 8
    for h in range(2):
        loads[2 * h].wait()
        loads[2 * h + 1].wait()

        def some_rows(g, carry):
            for i in range(group):
                r = h * half_rows + g * group + i
                q32 = qs[pl.ds(pl.multiple_of(r * heads, heads), heads), :]
                scores = dot_nt(q32.astype(BF), ck[r]) * score_scale
                own = jnp.sum(q32 * nk32[pl.ds(r, 1), :], axis=1, keepdims=True) * score_scale
                scores = jnp.where(position < len_ref[r], scores, -jnp.inf)
                highest = jnp.maximum(jnp.max(scores, axis=1, keepdims=True), own)
                e = jnp.exp(scores - highest)
                own_e = jnp.exp(own - highest)
                inv = 1.0 / (jnp.sum(e, axis=1, keepdims=True) + own_e)
                probs = (e * inv).astype(BF)
                own_p = (own_e * inv).astype(BF).astype(F32)
                o = jnp.dot(probs, cv[r], preferred_element_type=F32)
                o = o + own_p * nv32[pl.ds(r, 1), :]
                ao[pl.ds(pl.multiple_of(r * heads, heads), heads), :] = o
            return carry

        lax.fori_loop(0, half_rows // group, some_rows, 0)
        for j in range(heads):
            att[z, h * half_rows : (h + 1) * half_rows, j * HEAD_DIM : (j + 1) * HEAD_DIM] = ao[
                pl.ds(h * half_rows * heads + j, half_rows, stride=heads), :
            ].astype(BF)
        piece = att.at[z, pl.ds(h * half_rows, half_rows)]
        send(piece, piece, a_s.at[0, h], a_r.at[z, h], {"ep": z + 1}, z < N - 1)
        send(piece, piece, a_s.at[1, h], a_r.at[z, h], {"ep": z - 1}, z > 0)
        if h == 0:
            load_g = load(5, g_hbm, gw)
            load_u = load(6, u_hbm, uw)
            load_d = load(7, d_hbm, dw)
    load_wo.wait()

    for i in range(N):
        s = order[i]
        if i > 0:
            onward = jnp.where(s < z, z + 1, z - 1)
            go = jnp.logical_and(onward >= 0, onward < N)
            for h in range(2):
                piece = att.at[s, pl.ds(h * half_rows, half_rows)]
                arrived(piece, a_f.at[i, h], a_r.at[s, h])
                send(piece, piece, a_f.at[i, h], a_r.at[s, h], {"ep": onward}, go)

        def project(n, carry):
            cols = pl.ds(pl.multiple_of(n * quarter, quarter), quarter)
            part[i, n] = jnp.dot(att[s], wo[:, cols], preferred_element_type=F32)
            return carry

        lax.fori_loop(0, N, project, 0)

        @pl.when(t == z)
        def _():
            if i > 0:
                arrived(res_all.at[s], res_s.at[0], res_r.at[s])
                src = res_all.at[s]
            else:
                src = res_ref
            for n in range(N):
                part[i, n] = part[i, n] + src[:, n * quarter : (n + 1) * quarter].astype(F32)

        c1s[i] = part[i].astype(BF)
        for k in range(1, N):
            to = lax.rem(t + k, N)
            send(c1s.at[i, to], c1r.at[i, k - 1], c1_s.at[i, k], c1_rs.at[i, k], {"tp": to})
    my_gain = gain32[:, pl.ds(pl.multiple_of(z * width + t * quarter, quarter), quarter)]
    for i in range(N):
        s = order[i]
        total = part[i, t]
        for k in range(1, N):
            arrived(c1r.at[i, k - 1], c1_s.at[i, k], c1_rs.at[i, k])
            total = total + c1r[i, k - 1].astype(F32)
        hg[z, t, pl.ds(pl.multiple_of(s * rows, rows), rows), :] = (total * my_gain).astype(BF)

    load_g.wait()
    load_u.wait()
    for i in range(N):
        s = order[i]
        mine = hg.at[s, t]
        if i == 0:
            send(mine, mine, cz_s.at[0], cz_r.at[s], {"ep": z + 1}, z < N - 1)
            send(mine, mine, cz_s.at[1], cz_r.at[s], {"ep": z - 1}, z > 0)
        else:
            onward = jnp.where(s < z, z + 1, z - 1)
            go = jnp.logical_and(onward >= 0, onward < N)
            arrived(mine, cz_f.at[i], cz_r.at[s])
            send(mine, mine, cz_f.at[i], cz_r.at[s], {"ep": onward}, go)
        send(mine, mine, cx_s.at[i], cx_r.at[i], {"tp": t_x})
        send(mine, mine, cc_s.at[i, 0], cc_r.at[i, 0], {"tp": t_core})
        for j in ([i - 1] if i > 0 else []) + ([i] if i == N - 1 else []):
            sj = order[j]
            theirs = hg.at[sj, t_x]
            arrived(theirs, cx_s.at[j], cx_r.at[j])
            send(theirs, theirs, cc_s.at[j, 1], cc_r.at[j, 1], {"tp": t_core})
            arrived(hg.at[sj, t_core], cc_s.at[j, 0], cc_r.at[j, 0])
            arrived(hg.at[sj, t_diag], cc_s.at[j, 1], cc_r.at[j, 1])

            def gate_up(b, carry):
                cols = pl.ds(pl.multiple_of(sj * width + b * quarter, quarter), quarter)
                block = hg[sj, b]
                ga[...] += dot_nt(block, gw[:, cols])
                ua[...] += dot_nt(block, uw[:, cols])
                plain = block.astype(F32) * rgain[:, cols]
                square = plain * plain
                for m in range(quarter // 128):
                    ss[...] += square[:, m * 128 : (m + 1) * 128]
                return carry

            lax.fori_loop(0, N, gate_up, 0)

    units = ga.shape[1]
    per_expert = units // 2
    for i in range(1, N):
        s = order[i]
        arrived(w_all.at[s], w_s.at[i], w_r.at[s])
    unit = lax.broadcasted_iota(jnp.int32, (rows, units), 1)
    for s in range(N):
        at = slice(s * rows, (s + 1) * rows)
        mean_square = jnp.sum(ss[at], axis=1, keepdims=True) * (1.0 / (N * width))
        scale = lax.rsqrt(mean_square + 1e-06)
        dense = w_all[s]
        w0 = jnp.sum(jnp.where(lane == 2 * z, dense, 0.0), axis=1, keepdims=True)
        w1 = jnp.sum(jnp.where(lane == 2 * z + 1, dense, 0.0), axis=1, keepdims=True)
        gate = ga[at] * scale
        up = ua[at] * scale
        weight = jnp.where(unit < per_expert, w0, w1)
        act[at] = (gate / (1.0 + jnp.exp(-gate)) * up * weight).astype(BF)

    load_d.wait()
    for j, target in enumerate((t_diag, t_x, t_core, t)):

        def down(n, carry):
            cols = pl.ds(pl.multiple_of(target * width + n * quarter, quarter), quarter)
            to = pl.ds(pl.multiple_of(n * quarter, quarter), quarter)
            y = jnp.dot(act[...], dw[:, cols], preferred_element_type=F32)
            if j == 1:
                p1[:, to] = y
            elif j == 3:
                p3[:, to] = y
            else:
                ecs[j // 2, :, to] = y.astype(BF)
            return carry

        lax.fori_loop(0, N, down, 0)
        if j % 2 == 0:
            m = j // 2
            send(ecs.at[m], ecr.at[m], ec_s.at[m], ec_r.at[m], {"tp": t_core})
        if j == 1:
            arrived(ecr.at[0], ec_s.at[0], ec_r.at[0])
            for i in reversed(range(N)):
                s = order[i]
                at = pl.ds(pl.multiple_of(s * rows, rows), rows)
                xs[i] = (p1[at, :] + ecr[0, at, :].astype(F32)).astype(BF)
                send(xs.at[i], xr.at[i], ex_s.at[i], ex_r.at[i], {"tp": t_x})
    arrived(ecr.at[1], ec_s.at[1], ec_r.at[1])
    for i in reversed(range(N)):
        s = order[i]
        at = pl.ds(pl.multiple_of(s * rows, rows), rows)
        y = p3[at, :] + ecr[1, at, :].astype(F32)
        arrived(xr.at[i], ex_s.at[i], ex_r.at[i])
        y = y + xr[i].astype(F32)
        if i > 0:
            zs[i] = y.astype(BF)
            send(zs.at[i], zr.at[z], ez_s.at[i], ez_r.at[z], {"ep": s})
        else:
            for b in range(N):
                cols = pl.ds(pl.multiple_of(t * width + b * quarter, quarter), quarter)
                p1[:rows, b * quarter : (b + 1) * quarter] = (
                    y[:, b * quarter : (b + 1) * quarter]
                    + hg[t, b, pl.ds(pl.multiple_of(z * rows, rows), rows), :].astype(F32)
                    * rgain[:, cols]
                )
    total = p1[:rows, :]
    for i in range(1, N):
        s = order[i]
        arrived(zr.at[s], ez_s.at[i], ez_r.at[s])
        total = total + zr[s].astype(F32)
    out_ref[...] = total.astype(out_ref.dtype)

    for copy, cond in sends:
        if cond is None:
            copy.wait_send()
        else:
            pl.when(cond)(lambda copy=copy: copy.wait_send())


def dense_device(
    queries, cached_key_table, cached_value_table, fresh_token_keys, fresh_token_values, cache_len,
    out_proj, residual, norm_gain, routes, gate_weights, gate_proj, up_proj, down_proj,
):
    rows, heads = queries.shape[0], queries.shape[1] // HEAD_DIM
    width = residual.shape[1]
    quarter = width // N
    units = gate_proj.shape[0] * gate_proj.shape[1]
    all_width = N * width
    all_rows = N * rows
    flat = lambda w: w.reshape(units, all_width)
    vm, hbm = pl.BlockSpec(memory_space=pltpu.VMEM), pl.BlockSpec(memory_space=pl.ANY)
    smem = pl.BlockSpec(memory_space=pltpu.SMEM)
    V = pltpu.VMEM
    dma = pltpu.SemaphoreType.DMA
    scratch = [
        V(cached_key_table.shape, BF), V(cached_value_table.shape, BF), V(out_proj.shape, BF),
        V((units, all_width), BF), V((units, all_width), BF), V((units, all_width), BF),
        V((rows * heads, HEAD_DIM), F32), V((rows * heads, HEAD_DIM), F32),
        V((rows, HEAD_DIM), F32), V((rows, HEAD_DIM), F32),
        V((1, all_width), F32), V((1, all_width), F32),
        V((N, rows, heads * HEAD_DIM), BF), V((N, rows, width), BF), V((N, rows, 128), F32),
        V((N, N, rows, quarter), F32), V((N, N, rows, quarter), BF), V((N, N - 1, rows, quarter), BF),
        V((N, N, all_rows, quarter), BF), V((all_rows, units), F32), V((all_rows, units), F32),
        V((all_rows, 128), F32), V((all_rows, units), BF),
        V((2, all_rows, width), BF), V((2, all_rows, width), BF),
        V((all_rows, width), F32), V((all_rows, width), F32),
        V((N, rows, width), BF), V((N, rows, width), BF), V((N, rows, width), BF), V((N, rows, width), BF),
        dma((8,)), dma((1,)), dma((N,)), dma((N,)), dma((N,)),
        dma((2, 2)), dma((N, 2)), dma((N, 2)), dma((N, N)), dma((N, N)),
        dma((2,)), dma((N,)), dma((N,)), dma((N,)), dma((N,)), dma((N, 2)), dma((N, 2)),
        dma((2,)), dma((2,)), dma((N,)), dma((N,)), dma((N,)), dma((N,)),
    ]
    return pl.pallas_call(
        layer_kernel,
        out_shape=jax.ShapeDtypeStruct((rows, width), BF),
        in_specs=[smem, vm, hbm, hbm, vm, vm, hbm, vm, vm, vm, vm, hbm, hbm, hbm],
        out_specs=vm,
        scratch_shapes=scratch,
        compiler_params=pltpu.CompilerParams(
            collective_id=0, has_side_effects=True, vmem_limit_bytes=48 * 1024 * 1024
        ),
        name="layer",
    )(
        cache_len, queries, cached_key_table, cached_value_table, fresh_token_keys,
        fresh_token_values, out_proj, residual, norm_gain.reshape(1, -1), routes, gate_weights,
        flat(gate_proj), flat(up_proj), flat(down_proj),
    )


def pick_plan(mesh):
    def plan(*args):
        expert_count = args[11].shape[0] * mesh.shape["ep"]
        square = mesh.shape["ep"] == N and mesh.shape["tp"] == N
        one_kv_head = args[1].shape[2] == HEAD_DIM
        if square and one_kv_head and expert_count == TOP:
            return dense_device(*args)
        return per_device(*args)

    return plan


def solution(mesh):
    return jax.shard_map(
        pick_plan(mesh),
        mesh=mesh,
        in_specs=(
            P(("groups", "ep"), "tp"),
            P(("groups", "ep"), None, "tp"),
            P(("groups", "ep"), None, "tp"),
            P(("groups", "ep"), "tp"),
            P(("groups", "ep"), "tp"),
            P(("groups", "ep")),
            P("tp", "ep"),
            P(("groups", "ep"), "tp"),
            P(),
            P(("groups", "ep"), None),
            P(("groups", "ep"), None),
            P("ep", "tp", None),
            P("ep", "tp", None),
            P("ep", "tp", None),
        ),
        out_specs=P(("groups", "ep"), "tp"),
        check_vma=False,
    )
```

```python
import math

import jax
import jax.numpy as jnp
from jax import lax
from jax.experimental import pallas as pl
from jax.experimental.pallas import tpu as pltpu
from jax.sharding import PartitionSpec as P

HEAD_DIM = 128
TOP = 8


def attend_local(
    queries, cached_key_table, cached_value_table, fresh_token_keys, fresh_token_values, cache_len
):
    rows_here = queries.shape[0]
    kv_heads = cached_key_table.shape[2] // HEAD_DIM
    query_group_width = queries.shape[1] // HEAD_DIM // kv_heads
    cache_size = cached_key_table.shape[1]
    query_block = queries.reshape(rows_here, kv_heads, query_group_width, HEAD_DIM)
    key_block = cached_key_table.reshape(rows_here, cache_size, kv_heads, HEAD_DIM)
    value_block = cached_value_table.reshape(rows_here, cache_size, kv_heads, HEAD_DIM)
    newkey_block = fresh_token_keys.reshape(rows_here, kv_heads, HEAD_DIM)
    newval_block = fresh_token_values.reshape(rows_here, kv_heads, HEAD_DIM)
    score_scale = 1.0 / math.sqrt(HEAD_DIM)
    scores = (
        jnp.einsum("rkgd,rjkd->rkgj", query_block, key_block, preferred_element_type=jnp.float32)
        * score_scale
    )
    own_score = (
        jnp.einsum("rkgd,rkd->rkg", query_block, newkey_block, preferred_element_type=jnp.float32)
        * score_scale
    )
    usable = jnp.arange(cache_size, dtype=jnp.int32)[None, :] < cache_len[:, None]
    scores = jnp.where(usable[:, None, None, :], scores, -jnp.inf)
    highest = jnp.maximum(jnp.max(scores, axis=-1), own_score)
    exp_scores = jnp.exp(scores - highest[..., None])
    own_exp = jnp.exp(own_score - highest)
    denominator = jnp.sum(exp_scores, axis=-1) + own_exp
    attn_probs = (exp_scores / denominator[..., None]).astype(jnp.bfloat16)
    own_prob = (own_exp / denominator).astype(jnp.bfloat16)
    attended = jnp.einsum(
        "rkgj,rjkd->rkgd", attn_probs, value_block, preferred_element_type=jnp.float32
    )
    attended = (
        attended
        + own_prob.astype(jnp.float32)[..., None] * newval_block.astype(jnp.float32)[:, :, None, :]
    )
    return attended.reshape(rows_here, -1).astype(jnp.bfloat16)


def per_device(
    queries,
    cached_key_table,
    cached_value_table,
    fresh_token_keys,
    fresh_token_values,
    cache_len,
    out_proj,
    residual,
    norm_gain,
    routes,
    gate_weights,
    gate_proj,
    up_proj,
    down_proj,
):
    attended = attend_local(
        queries,
        cached_key_table,
        cached_value_table,
        fresh_token_keys,
        fresh_token_values,
        cache_len,
    )
    partial_all = jnp.dot(
        lax.all_gather(attended, "ep", axis=0, tiled=True),
        out_proj,
        preferred_element_type=jnp.float32,
    )
    partial_rows = lax.all_to_all(partial_all, "ep", split_axis=0, concat_axis=1, tiled=True)
    ep_count = lax.axis_size("ep")
    tp_index = lax.axis_index("tp")
    rows_here = residual.shape[0]
    col_width = residual.shape[1]
    local_experts = gate_proj.shape[0]
    expert_count = local_experts * ep_count
    capacity = min(rows_here, 2 * rows_here * TOP // expert_count)
    flat_routes = routes.reshape(-1)
    pair_count = flat_routes.shape[0]
    member = (flat_routes[:, None] == jnp.arange(expert_count, dtype=jnp.int32)[None, :]).astype(
        jnp.int32
    )
    earlier = jnp.cumsum(member, axis=0) - member
    position = jnp.sum(earlier * member, axis=1)
    target = flat_routes * capacity + position
    slot_match = (
        jnp.arange(expert_count * capacity, dtype=jnp.int32)[:, None] == target[None, :]
    ).astype(jnp.int32)
    occupied = jnp.sum(slot_match, axis=1)
    source_row = jnp.sum(
        slot_match * (jnp.arange(pair_count, dtype=jnp.int32) // TOP)[None, :], axis=1
    )
    gain_full = norm_gain.astype(jnp.float32)
    own_cols = lax.dynamic_slice_in_dim(
        partial_rows, tp_index * col_width, col_width, 1
    ) + residual.astype(jnp.float32)
    with_residual = lax.dynamic_update_slice_in_dim(partial_rows, own_cols, tp_index * col_width, 1)
    hidden_full = lax.psum(with_residual, "tp")
    mean_square = jnp.mean(hidden_full * hidden_full, axis=-1, keepdims=True)
    normed = (hidden_full * lax.rsqrt(mean_square + 1e-06) * gain_full).astype(jnp.bfloat16)
    hidden = lax.dynamic_slice_in_dim(hidden_full, tp_index * col_width, col_width, 1)
    picked = jnp.where(occupied[:, None] > 0, normed[source_row], jnp.zeros((), normed.dtype))
    arrived = lax.all_to_all(
        picked.reshape(ep_count, local_experts, capacity, normed.shape[1]),
        "ep",
        split_axis=0,
        concat_axis=0,
        tiled=True,
    )
    gate_part = jnp.einsum("aesd,efd->aesf", arrived, gate_proj, preferred_element_type=jnp.float32)
    up_part = jnp.einsum("aesd,efd->aesf", arrived, up_proj, preferred_element_type=jnp.float32)
    activated = (jax.nn.silu(gate_part) * up_part).astype(jnp.bfloat16)
    partial_out = jnp.einsum(
        "aesf,efd->aesd", activated, down_proj, preferred_element_type=jnp.float32
    )
    reduced = lax.psum_scatter(
        partial_out.astype(jnp.bfloat16), "tp", scatter_dimension=3, tiled=True
    ).astype(jnp.float32)
    returned = lax.all_to_all(
        reduced.astype(jnp.bfloat16), "ep", split_axis=0, concat_axis=0, tiled=True
    ).astype(reduced.dtype)
    flat_back = returned.reshape(expert_count * capacity, col_width)
    pair_out = flat_back[target].reshape(rows_here, TOP, col_width)
    mixture = jnp.sum(gate_weights[:, :, None] * pair_out, axis=1)
    return (hidden + mixture).astype(jnp.bfloat16)


MESH = pl.DeviceIdType.MESH
N = 4
BF = jnp.bfloat16
F32 = jnp.float32


def dot_nt(a, b):
    return lax.dot_general(a, b, (((1,), (1,)), ((), ())), preferred_element_type=F32)


def layer_kernel(
    len_hbm, q_hbm, ck_hbm, cv_hbm, nk_hbm, nv_hbm, wo_hbm, res_hbm, gain_hbm, routes_hbm, gw_hbm,
    g_hbm, u_hbm, d_hbm, out_ref,
    len_ref, q_ref, nk_ref, nv_ref, res_ref, gain_ref, routes_ref, gw_ref, ck, cv, wo, gw, uw, dw, qs, ao, nk32, nv32, gain32, rgain, att, res_all, w_all,
    part, c1s, c1r, hg, ga, ua, ss, act, ecs, ecr, p1, p3, xs, xr, zs, zr,
    load_sem, res_s, res_r, w_s, w_r, a_s, a_f, a_r, c1_s, c1_rs, cz_s, cz_f, cz_r, cx_s, cx_r,
    cc_s, cc_r, ec_s, ec_r, ex_s, ex_r, ez_s, ez_r,
):
    rows, heads = q_ref.shape[0], q_ref.shape[1] // HEAD_DIM
    slots = ck.shape[1]
    width = res_ref.shape[1]
    quarter = width // N
    half_rows = rows // 2
    z = lax.axis_index("ep")
    t = lax.axis_index("tp")
    core, xpos = lax.rem(t, 2), t // 2
    t_core = 2 * xpos + (1 - core)
    t_x = 2 * (1 - xpos) + core
    t_diag = 2 * (1 - xpos) + (1 - core)
    order = [
        z,
        jnp.where(z == 0, 1, z - 1),
        jnp.where(z == 0, 2, jnp.where(z == N - 1, 1, z + 1)),
        jnp.where(z <= 1, 3, 0),
    ]
    always = z >= 0
    sends = []

    def load(i, src, dst):
        copy = pltpu.make_async_copy(src, dst, load_sem.at[i])
        copy.start()
        return copy

    def send(src, dst, s_sem, r_sem, where, cond=None):
        copy = pltpu.make_async_remote_copy(
            src_ref=src, dst_ref=dst, send_sem=s_sem, recv_sem=r_sem, device_id=where,
            device_id_type=MESH,
        )
        if cond is None:
            copy.start()
        else:
            pl.when(cond)(lambda: copy.start())
        sends.append((copy, cond))

    def arrived(dst, s_sem, r_sem):
        pltpu.make_async_remote_copy(
            src_ref=dst, dst_ref=dst, send_sem=s_sem, recv_sem=r_sem, device_id={"ep": z},
            device_id_type=MESH,
        ).wait_recv()

    load_q = load(8, q_hbm, q_ref)
    loads = []
    for h in range(2):
        piece = pl.ds(h * half_rows, half_rows)
        loads.append(load(2 * h, ck_hbm.at[piece], ck.at[piece]))
        loads.append(load(2 * h + 1, cv_hbm.at[piece], cv.at[piece]))
    pairs = (
        (len_hbm, len_ref), (nk_hbm, nk_ref), (nv_hbm, nv_ref), (res_hbm, res_ref),
        (gain_hbm, gain_ref), (routes_hbm, routes_ref), (gw_hbm, gw_ref),
    )
    small = [load(9 + i, src, dst) for i, (src, dst) in enumerate(pairs)]

    barrier = pltpu.get_barrier_semaphore()
    for k in range(1, N):
        pl.semaphore_signal(barrier, inc=1, device_id={"ep": lax.rem(z + k, N)}, device_id_type=MESH)
        pl.semaphore_signal(barrier, inc=1, device_id={"tp": lax.rem(t + k, N)}, device_id_type=MESH)

    ga[...] = jnp.zeros_like(ga)
    ua[...] = jnp.zeros_like(ua)
    ss[...] = jnp.zeros_like(ss)
    for copy in small:
        copy.wait()
    lane = lax.broadcasted_iota(jnp.int32, (rows, 128), 1)
    routes = jnp.transpose(routes_ref[...])
    weights = jnp.transpose(gw_ref[...])
    dense = jnp.zeros((rows, 128), F32)
    for k in range(TOP):
        dense = dense + jnp.where(lane == routes[:, k : k + 1], weights[:, k : k + 1], 0.0)
    w_all[z] = dense
    load_q.wait()
    for h in range(heads):
        qs[pl.ds(h, rows, stride=heads), :] = q_ref[:, h * HEAD_DIM : (h + 1) * HEAD_DIM].astype(F32)
    nk32[...] = nk_ref[...].astype(F32)
    nv32[...] = nv_ref[...].astype(F32)
    gain = gain_ref[...].astype(F32)
    for j in range(gain.shape[0]):
        gain32[:, j * 128 : (j + 1) * 128] = gain[j : j + 1, :]
    rgain[...] = 1.0 / gain32[...]

    score_scale = 1.0 / math.sqrt(HEAD_DIM)
    position = lax.broadcasted_iota(jnp.int32, (heads, slots), 1)
    group = 8
    for h in range(2):
        loads[2 * h].wait()
        loads[2 * h + 1].wait()
        if h == 0:
            load_wo = load(4, wo_hbm, wo)

        def some_rows(g, carry):
            first = h * half_rows + g * group
            at = pl.ds(pl.multiple_of(first * heads, group * heads), group * heads)
            q32 = qs[at, :]
            q16 = q32.astype(BF)
            scores, fresh_k, fresh_v = [], [], []
            for i in range(group):
                one = q16[i * heads : (i + 1) * heads]
                dots = dot_nt(one, ck[first + i]) * score_scale
                scores.append(jnp.where(position < len_ref[first + i], dots, -jnp.inf))
                fresh_k.append(jnp.broadcast_to(nk32[pl.ds(first + i, 1), :], (heads, HEAD_DIM)))
                fresh_v.append(jnp.broadcast_to(nv32[pl.ds(first + i, 1), :], (heads, HEAD_DIM)))
            scores = jnp.concatenate(scores, axis=0)
            own = jnp.sum(q32 * jnp.concatenate(fresh_k, axis=0), axis=1, keepdims=True) * score_scale
            highest = jnp.maximum(jnp.max(scores, axis=1, keepdims=True), own)
            e = jnp.exp(scores - highest)
            own_e = jnp.exp(own - highest)
            inv = 1.0 / (jnp.sum(e, axis=1, keepdims=True) + own_e)
            probs = (e * inv).astype(BF)
            own_p = (own_e * inv).astype(BF).astype(F32)
            o = [
                jnp.dot(probs[i * heads : (i + 1) * heads], cv[first + i], preferred_element_type=F32)
                for i in range(group)
            ]
            ao[at, :] = jnp.concatenate(o, axis=0) + own_p * jnp.concatenate(fresh_v, axis=0)
            return carry

        lax.fori_loop(0, half_rows // group, some_rows, 0)
        for j in range(heads):
            att[z, h * half_rows : (h + 1) * half_rows, j * HEAD_DIM : (j + 1) * HEAD_DIM] = ao[
                pl.ds(h * half_rows * heads + j, half_rows, stride=heads), :
            ].astype(BF)
        if h == 0:
            pl.semaphore_wait(barrier, 2 * (N - 1))
        piece = att.at[z, pl.ds(h * half_rows, half_rows)]
        send(piece, piece, a_s.at[0, h], a_r.at[z, h], {"ep": z + 1}, z < N - 1)
        send(piece, piece, a_s.at[1, h], a_r.at[z, h], {"ep": z - 1}, z > 0)
        if h == 0:
            load_g = load(5, g_hbm, gw)
            load_u = load(6, u_hbm, uw)
            load_d = load(7, d_hbm, dw)
            send(res_ref, res_all.at[z], res_s.at[0], res_r.at[z], {"ep": t}, z != t)
            for k in range(1, N):
                send(w_all.at[z], w_all.at[z], w_s.at[k], w_r.at[z], {"ep": lax.rem(z + k, N)})
    load_wo.wait()

    for i in range(N):
        s = order[i]
        if i > 0:
            onward = jnp.where(s < z, z + 1, z - 1)
            go = jnp.logical_and(onward >= 0, onward < N)
            for h in range(2):
                piece = att.at[s, pl.ds(h * half_rows, half_rows)]
                arrived(piece, a_f.at[i, h], a_r.at[s, h])
                send(piece, piece, a_f.at[i, h], a_r.at[s, h], {"ep": onward}, go)

        def project(n, carry):
            cols = pl.ds(pl.multiple_of(n * quarter, quarter), quarter)
            part[i, n] = jnp.dot(att[s], wo[:, cols], preferred_element_type=F32)
            return carry

        lax.fori_loop(0, N, project, 0)

        @pl.when(t == z)
        def _():
            if i > 0:
                arrived(res_all.at[s], res_s.at[0], res_r.at[s])
                src = res_all.at[s]
            else:
                src = res_ref
            for n in range(N):
                part[i, n] = part[i, n] + src[:, n * quarter : (n + 1) * quarter].astype(F32)

        c1s[i] = part[i].astype(BF)
        for k in range(1, N):
            to = lax.rem(t + k, N)
            send(c1s.at[i, to], c1r.at[i, k - 1], c1_s.at[i, k], c1_rs.at[i, k], {"tp": to})
    my_gain = gain32[:, pl.ds(pl.multiple_of(z * width + t * quarter, quarter), quarter)]
    for i in range(N):
        s = order[i]
        total = part[i, t]
        for k in range(1, N):
            arrived(c1r.at[i, k - 1], c1_s.at[i, k], c1_rs.at[i, k])
            total = total + c1r[i, k - 1].astype(F32)
        hg[z, t, pl.ds(pl.multiple_of(s * rows, rows), rows), :] = (total * my_gain).astype(BF)

    load_g.wait()
    load_u.wait()
    for i in range(N):
        s = order[i]
        mine = hg.at[s, t]
        if i == 0:
            send(mine, mine, cz_s.at[0], cz_r.at[s], {"ep": z + 1}, z < N - 1)
            send(mine, mine, cz_s.at[1], cz_r.at[s], {"ep": z - 1}, z > 0)
        else:
            onward = jnp.where(s < z, z + 1, z - 1)
            go = jnp.logical_and(onward >= 0, onward < N)
            arrived(mine, cz_f.at[i], cz_r.at[s])
            send(mine, mine, cz_f.at[i], cz_r.at[s], {"ep": onward}, go)
        send(mine, mine, cx_s.at[i], cx_r.at[i], {"tp": t_x})
        send(mine, mine, cc_s.at[i, 0], cc_r.at[i, 0], {"tp": t_core})
        for j in ([i - 1] if i > 0 else []) + ([i] if i == N - 1 else []):
            sj = order[j]
            theirs = hg.at[sj, t_x]
            arrived(theirs, cx_s.at[j], cx_r.at[j])
            send(theirs, theirs, cc_s.at[j, 1], cc_r.at[j, 1], {"tp": t_core})
            arrived(hg.at[sj, t_core], cc_s.at[j, 0], cc_r.at[j, 0])
            arrived(hg.at[sj, t_diag], cc_s.at[j, 1], cc_r.at[j, 1])

            def gate_up(b, carry):
                cols = pl.ds(pl.multiple_of(sj * width + b * quarter, quarter), quarter)
                block = hg[sj, b]
                ga[...] += dot_nt(block, gw[:, cols])
                ua[...] += dot_nt(block, uw[:, cols])
                plain = block.astype(F32) * rgain[:, cols]
                square = plain * plain
                for m in range(quarter // 128):
                    ss[...] += square[:, m * 128 : (m + 1) * 128]
                return carry

            lax.fori_loop(0, N, gate_up, 0)

    units = ga.shape[1]
    per_expert = units // 2
    for i in range(1, N):
        s = order[i]
        arrived(w_all.at[s], w_s.at[i], w_r.at[s])
    unit = lax.broadcasted_iota(jnp.int32, (rows, units), 1)
    for s in range(N):
        at = slice(s * rows, (s + 1) * rows)
        mean_square = jnp.sum(ss[at], axis=1, keepdims=True) * (1.0 / (N * width))
        scale = lax.rsqrt(mean_square + 1e-06)
        dense = w_all[s]
        w0 = jnp.sum(jnp.where(lane == 2 * z, dense, 0.0), axis=1, keepdims=True)
        w1 = jnp.sum(jnp.where(lane == 2 * z + 1, dense, 0.0), axis=1, keepdims=True)
        gate = ga[at] * scale
        up = ua[at] * scale
        weight = jnp.where(unit < per_expert, w0, w1)
        act[at] = (gate / (1.0 + jnp.exp(-gate)) * up * weight).astype(BF)

    load_d.wait()
    for j, target in enumerate((t_diag, t_x, t_core, t)):

        def down(n, carry):
            cols = pl.ds(pl.multiple_of(target * width + n * quarter, quarter), quarter)
            to = pl.ds(pl.multiple_of(n * quarter, quarter), quarter)
            y = jnp.dot(act[...], dw[:, cols], preferred_element_type=F32)
            if j == 1:
                p1[:, to] = y
            elif j == 3:
                p3[:, to] = y
            else:
                ecs[j // 2, :, to] = y.astype(BF)
            return carry

        lax.fori_loop(0, N, down, 0)
        if j % 2 == 0:
            m = j // 2
            send(ecs.at[m], ecr.at[m], ec_s.at[m], ec_r.at[m], {"tp": t_core})
        if j == 1:
            arrived(ecr.at[0], ec_s.at[0], ec_r.at[0])
            for i in reversed(range(N)):
                s = order[i]
                at = pl.ds(pl.multiple_of(s * rows, rows), rows)
                xs[i] = (p1[at, :] + ecr[0, at, :].astype(F32)).astype(BF)
                send(xs.at[i], xr.at[i], ex_s.at[i], ex_r.at[i], {"tp": t_x})
    arrived(ecr.at[1], ec_s.at[1], ec_r.at[1])
    for i in reversed(range(N)):
        s = order[i]
        at = pl.ds(pl.multiple_of(s * rows, rows), rows)
        y = p3[at, :] + ecr[1, at, :].astype(F32)
        arrived(xr.at[i], ex_s.at[i], ex_r.at[i])
        y = y + xr[i].astype(F32)
        if i > 0:
            zs[i] = y.astype(BF)
            send(zs.at[i], zr.at[z], ez_s.at[i], ez_r.at[z], {"ep": s})
        else:
            for b in range(N):
                cols = pl.ds(pl.multiple_of(t * width + b * quarter, quarter), quarter)
                p1[:rows, b * quarter : (b + 1) * quarter] = (
                    y[:, b * quarter : (b + 1) * quarter]
                    + hg[t, b, pl.ds(pl.multiple_of(z * rows, rows), rows), :].astype(F32)
                    * rgain[:, cols]
                )
    total = p1[:rows, :]
    for i in range(1, N):
        s = order[i]
        arrived(zr.at[s], ez_s.at[i], ez_r.at[s])
        total = total + zr[s].astype(F32)
    out_ref[...] = total.astype(out_ref.dtype)

    for copy, cond in sends:
        if cond is None:
            copy.wait_send()
        else:
            pl.when(cond)(lambda copy=copy: copy.wait_send())


def dense_device(
    queries, cached_key_table, cached_value_table, fresh_token_keys, fresh_token_values, cache_len,
    out_proj, residual, norm_gain, routes, gate_weights, gate_proj, up_proj, down_proj,
):
    rows, heads = queries.shape[0], queries.shape[1] // HEAD_DIM
    width = residual.shape[1]
    quarter = width // N
    units = gate_proj.shape[0] * gate_proj.shape[1]
    all_width = N * width
    all_rows = N * rows
    flat = lambda w: w.reshape(units, all_width)
    vm, hbm = pl.BlockSpec(memory_space=pltpu.VMEM), pl.BlockSpec(memory_space=pltpu.HBM)
    V = pltpu.VMEM
    dma = pltpu.SemaphoreType.DMA
    gain = norm_gain.reshape(-1, 128)
    scratch = [
        pltpu.SMEM(cache_len.shape, jnp.int32), V(queries.shape, BF),
        V(fresh_token_keys.shape, BF), V(fresh_token_values.shape, BF), V(residual.shape, BF),
        V(gain.shape, BF), V((TOP, rows), jnp.int32), V((TOP, rows), F32),
        V(cached_key_table.shape, BF), V(cached_value_table.shape, BF), V(out_proj.shape, BF),
        V((units, all_width), BF), V((units, all_width), BF), V((units, all_width), BF),
        V((rows * heads, HEAD_DIM), F32), V((rows * heads, HEAD_DIM), F32),
        V((rows, HEAD_DIM), F32), V((rows, HEAD_DIM), F32),
        V((1, all_width), F32), V((1, all_width), F32),
        V((N, rows, heads * HEAD_DIM), BF), V((N, rows, width), BF), V((N, rows, 128), F32),
        V((N, N, rows, quarter), F32), V((N, N, rows, quarter), BF), V((N, N - 1, rows, quarter), BF),
        V((N, N, all_rows, quarter), BF), V((all_rows, units), F32), V((all_rows, units), F32),
        V((all_rows, 128), F32), V((all_rows, units), BF),
        V((2, all_rows, width), BF), V((2, all_rows, width), BF),
        V((all_rows, width), F32), V((all_rows, width), F32),
        V((N, rows, width), BF), V((N, rows, width), BF), V((N, rows, width), BF), V((N, rows, width), BF),
        dma((16,)), dma((1,)), dma((N,)), dma((N,)), dma((N,)),
        dma((2, 2)), dma((N, 2)), dma((N, 2)), dma((N, N)), dma((N, N)),
        dma((2,)), dma((N,)), dma((N,)), dma((N,)), dma((N,)), dma((N, 2)), dma((N, 2)),
        dma((2,)), dma((2,)), dma((N,)), dma((N,)), dma((N,)), dma((N,)),
    ]
    return pl.pallas_call(
        layer_kernel,
        out_shape=jax.ShapeDtypeStruct((rows, width), BF),
        in_specs=[hbm] * 14,
        out_specs=vm,
        scratch_shapes=scratch,
        compiler_params=pltpu.CompilerParams(
            collective_id=0, has_side_effects=True, vmem_limit_bytes=63 * 1024 * 1024
        ),
        name="layer",
    )(
        cache_len, queries, cached_key_table, cached_value_table, fresh_token_keys,
        fresh_token_values, out_proj, residual, gain, routes.T, gate_weights.T,
        flat(gate_proj), flat(up_proj), flat(down_proj),
    )


def pick_plan(mesh):
    def plan(*args):
        expert_count = args[11].shape[0] * mesh.shape["ep"]
        square = mesh.shape["ep"] == N and mesh.shape["tp"] == N
        one_kv_head = args[1].shape[2] == HEAD_DIM
        if square and one_kv_head and expert_count == TOP:
            return dense_device(*args)
        return per_device(*args)

    return plan


def solution(mesh):
    return jax.shard_map(
        pick_plan(mesh),
        mesh=mesh,
        in_specs=(
            P(("groups", "ep"), "tp"),
            P(("groups", "ep"), None, "tp"),
            P(("groups", "ep"), None, "tp"),
            P(("groups", "ep"), "tp"),
            P(("groups", "ep"), "tp"),
            P(("groups", "ep")),
            P("tp", "ep"),
            P(("groups", "ep"), "tp"),
            P(),
            P(("groups", "ep"), None),
            P(("groups", "ep"), None),
            P("ep", "tp", None),
            P("ep", "tp", None),
            P("ep", "tp", None),
        ),
        out_specs=P(("groups", "ep"), "tp"),
        check_vma=False,
    )
```

```python
import math

import jax
import jax.numpy as jnp
from jax import lax
from jax.experimental import pallas as pl
from jax.experimental.pallas import tpu as pltpu
from jax.sharding import PartitionSpec as P

HEAD_DIM = 128
TOP = 8


def attend_local(
    queries, cached_key_table, cached_value_table, fresh_token_keys, fresh_token_values, cache_len
):
    rows_here = queries.shape[0]
    kv_heads = cached_key_table.shape[2] // HEAD_DIM
    query_group_width = queries.shape[1] // HEAD_DIM // kv_heads
    cache_size = cached_key_table.shape[1]
    query_block = queries.reshape(rows_here, kv_heads, query_group_width, HEAD_DIM)
    key_block = cached_key_table.reshape(rows_here, cache_size, kv_heads, HEAD_DIM)
    value_block = cached_value_table.reshape(rows_here, cache_size, kv_heads, HEAD_DIM)
    newkey_block = fresh_token_keys.reshape(rows_here, kv_heads, HEAD_DIM)
    newval_block = fresh_token_values.reshape(rows_here, kv_heads, HEAD_DIM)
    score_scale = 1.0 / math.sqrt(HEAD_DIM)
    scores = (
        jnp.einsum("rkgd,rjkd->rkgj", query_block, key_block, preferred_element_type=jnp.float32)
        * score_scale
    )
    own_score = (
        jnp.einsum("rkgd,rkd->rkg", query_block, newkey_block, preferred_element_type=jnp.float32)
        * score_scale
    )
    usable = jnp.arange(cache_size, dtype=jnp.int32)[None, :] < cache_len[:, None]
    scores = jnp.where(usable[:, None, None, :], scores, -jnp.inf)
    highest = jnp.maximum(jnp.max(scores, axis=-1), own_score)
    exp_scores = jnp.exp(scores - highest[..., None])
    own_exp = jnp.exp(own_score - highest)
    denominator = jnp.sum(exp_scores, axis=-1) + own_exp
    attn_probs = (exp_scores / denominator[..., None]).astype(jnp.bfloat16)
    own_prob = (own_exp / denominator).astype(jnp.bfloat16)
    attended = jnp.einsum(
        "rkgj,rjkd->rkgd", attn_probs, value_block, preferred_element_type=jnp.float32
    )
    attended = (
        attended
        + own_prob.astype(jnp.float32)[..., None] * newval_block.astype(jnp.float32)[:, :, None, :]
    )
    return attended.reshape(rows_here, -1).astype(jnp.bfloat16)


def per_device(
    queries,
    cached_key_table,
    cached_value_table,
    fresh_token_keys,
    fresh_token_values,
    cache_len,
    out_proj,
    residual,
    norm_gain,
    routes,
    gate_weights,
    gate_proj,
    up_proj,
    down_proj,
):
    attended = attend_local(
        queries,
        cached_key_table,
        cached_value_table,
        fresh_token_keys,
        fresh_token_values,
        cache_len,
    )
    partial_all = jnp.dot(
        lax.all_gather(attended, "ep", axis=0, tiled=True),
        out_proj,
        preferred_element_type=jnp.float32,
    )
    partial_rows = lax.all_to_all(partial_all, "ep", split_axis=0, concat_axis=1, tiled=True)
    ep_count = lax.axis_size("ep")
    tp_index = lax.axis_index("tp")
    rows_here = residual.shape[0]
    col_width = residual.shape[1]
    local_experts = gate_proj.shape[0]
    expert_count = local_experts * ep_count
    capacity = min(rows_here, 2 * rows_here * TOP // expert_count)
    flat_routes = routes.reshape(-1)
    pair_count = flat_routes.shape[0]
    member = (flat_routes[:, None] == jnp.arange(expert_count, dtype=jnp.int32)[None, :]).astype(
        jnp.int32
    )
    earlier = jnp.cumsum(member, axis=0) - member
    position = jnp.sum(earlier * member, axis=1)
    target = flat_routes * capacity + position
    slot_match = (
        jnp.arange(expert_count * capacity, dtype=jnp.int32)[:, None] == target[None, :]
    ).astype(jnp.int32)
    occupied = jnp.sum(slot_match, axis=1)
    source_row = jnp.sum(
        slot_match * (jnp.arange(pair_count, dtype=jnp.int32) // TOP)[None, :], axis=1
    )
    gain_full = norm_gain.astype(jnp.float32)
    own_cols = lax.dynamic_slice_in_dim(
        partial_rows, tp_index * col_width, col_width, 1
    ) + residual.astype(jnp.float32)
    with_residual = lax.dynamic_update_slice_in_dim(partial_rows, own_cols, tp_index * col_width, 1)
    hidden_full = lax.psum(with_residual, "tp")
    mean_square = jnp.mean(hidden_full * hidden_full, axis=-1, keepdims=True)
    normed = (hidden_full * lax.rsqrt(mean_square + 1e-06) * gain_full).astype(jnp.bfloat16)
    hidden = lax.dynamic_slice_in_dim(hidden_full, tp_index * col_width, col_width, 1)
    picked = jnp.where(occupied[:, None] > 0, normed[source_row], jnp.zeros((), normed.dtype))
    arrived = lax.all_to_all(
        picked.reshape(ep_count, local_experts, capacity, normed.shape[1]),
        "ep",
        split_axis=0,
        concat_axis=0,
        tiled=True,
    )
    gate_part = jnp.einsum("aesd,efd->aesf", arrived, gate_proj, preferred_element_type=jnp.float32)
    up_part = jnp.einsum("aesd,efd->aesf", arrived, up_proj, preferred_element_type=jnp.float32)
    activated = (jax.nn.silu(gate_part) * up_part).astype(jnp.bfloat16)
    partial_out = jnp.einsum(
        "aesf,efd->aesd", activated, down_proj, preferred_element_type=jnp.float32
    )
    reduced = lax.psum_scatter(
        partial_out.astype(jnp.bfloat16), "tp", scatter_dimension=3, tiled=True
    ).astype(jnp.float32)
    returned = lax.all_to_all(
        reduced.astype(jnp.bfloat16), "ep", split_axis=0, concat_axis=0, tiled=True
    ).astype(reduced.dtype)
    flat_back = returned.reshape(expert_count * capacity, col_width)
    pair_out = flat_back[target].reshape(rows_here, TOP, col_width)
    mixture = jnp.sum(gate_weights[:, :, None] * pair_out, axis=1)
    return (hidden + mixture).astype(jnp.bfloat16)


MESH = pl.DeviceIdType.MESH
N = 4
BF = jnp.bfloat16
F32 = jnp.float32


def dot_nt(a, b):
    return lax.dot_general(a, b, (((1,), (1,)), ((), ())), preferred_element_type=F32)


def layer_kernel(
    len_hbm, q_hbm, ck_hbm, cv_hbm, nk_hbm, nv_hbm, wo_hbm, res_hbm, gain_hbm, routes_hbm, gw_hbm,
    g_hbm, u_hbm, d_hbm, out_ref,
    len_ref, q_ref, nk_ref, nv_ref, res_ref, gain_ref, routes_ref, gw_ref, ck, cv, wo, gw, uw, dw, qs, ao, nk32, nv32, gain32, rgain, att, res_all, w_all,
    part, c1s, c1r, hg, ga, ua, ss, act, ecs, ecr, p1, p3, xs, xr, zs, zr, wsum,
    load_sem, res_s, res_r, w_s, w_r, a_s, a_f, a_r, c1_s, c1_rs, cz_s, cz_r, cx_s, cx_r,
    cc_s, cc_r, ec_s, ec_r, ex_s, ex_r, ez_s, ez_r,
):
    rows, heads = q_ref.shape[0], q_ref.shape[1] // HEAD_DIM
    slots = ck.shape[1]
    width = res_ref.shape[1]
    quarter = width // N
    half_rows = rows // 2
    z = lax.axis_index("ep")
    t = lax.axis_index("tp")
    core, xpos = lax.rem(t, 2), t // 2
    t_core = 2 * xpos + (1 - core)
    t_x = 2 * (1 - xpos) + core
    t_diag = 2 * (1 - xpos) + (1 - core)
    order = [
        z,
        jnp.where(z == 0, 1, z - 1),
        jnp.where(z == 0, 2, jnp.where(z == N - 1, 1, z + 1)),
        jnp.where(z <= 1, 3, 0),
    ]
    always = z >= 0
    sends = []

    def load(i, src, dst):
        copy = pltpu.make_async_copy(src, dst, load_sem.at[i])
        copy.start()
        return copy

    def send(src, dst, s_sem, r_sem, where, cond=None):
        copy = pltpu.make_async_remote_copy(
            src_ref=src, dst_ref=dst, send_sem=s_sem, recv_sem=r_sem, device_id=where,
            device_id_type=MESH,
        )
        if cond is None:
            copy.start()
        else:
            pl.when(cond)(lambda: copy.start())
        sends.append((copy, cond))

    def arrived(dst, s_sem, r_sem):
        pltpu.make_async_remote_copy(
            src_ref=dst, dst_ref=dst, send_sem=s_sem, recv_sem=r_sem, device_id={"ep": z},
            device_id_type=MESH,
        ).wait_recv()

    load_q = load(8, q_hbm, q_ref)
    loads = []
    for h in range(2):
        piece = pl.ds(h * half_rows, half_rows)
        loads.append(load(2 * h, ck_hbm.at[piece], ck.at[piece]))
        loads.append(load(2 * h + 1, cv_hbm.at[piece], cv.at[piece]))
    pairs = (
        (len_hbm, len_ref), (nk_hbm, nk_ref), (nv_hbm, nv_ref), (res_hbm, res_ref),
        (gain_hbm, gain_ref), (routes_hbm, routes_ref), (gw_hbm, gw_ref),
    )
    small = [load(9 + i, src, dst) for i, (src, dst) in enumerate(pairs)]

    barrier = pltpu.get_barrier_semaphore()
    for k in range(1, N):
        pl.semaphore_signal(barrier, inc=1, device_id={"ep": lax.rem(z + k, N)}, device_id_type=MESH)
        pl.semaphore_signal(barrier, inc=1, device_id={"tp": lax.rem(t + k, N)}, device_id_type=MESH)

    ga[...] = jnp.zeros_like(ga)
    ua[...] = jnp.zeros_like(ua)
    ss[...] = jnp.zeros_like(ss)
    for copy in small:
        copy.wait()
    expert = lax.broadcasted_iota(jnp.int32, (TOP, rows), 0)
    dense = jnp.zeros((TOP, rows), F32)
    for k in range(TOP):
        dense = dense + jnp.where(expert == routes_ref[k : k + 1, :], gw_ref[k : k + 1, :], 0.0)
    owner = lax.broadcasted_iota(jnp.int32, (TOP, N * rows), 1) // rows
    dense = jnp.where(owner == z, jnp.concatenate([dense] * N, axis=1), 0.0)
    w_all[z] = dense
    load_q.wait()
    for h in range(heads):
        qs[pl.ds(h, rows, stride=heads), :] = q_ref[:, h * HEAD_DIM : (h + 1) * HEAD_DIM].astype(F32)
    nk32[...] = nk_ref[...].astype(F32)
    nv32[...] = nv_ref[...].astype(F32)
    gain = gain_ref[...].astype(F32)
    for j in range(gain.shape[0]):
        gain32[:, j * 128 : (j + 1) * 128] = gain[j : j + 1, :]
    rgain[...] = 1.0 / gain32[...]

    score_scale = 1.0 / math.sqrt(HEAD_DIM)
    group = 8
    position = lax.broadcasted_iota(jnp.int32, (slots, group * heads), 0)
    lane_row = lax.broadcasted_iota(jnp.int32, (1, group * heads), 1) // heads
    own_block = lax.broadcasted_iota(jnp.int32, (group, group * heads), 0) == lane_row
    for h in range(2):
        loads[2 * h].wait()
        loads[2 * h + 1].wait()
        if h == 0:
            load_wo = load(4, wo_hbm, wo)

        def some_rows(g, carry):
            first = h * half_rows + g * group
            at = pl.ds(pl.multiple_of(first * heads, group * heads), group * heads)
            q16 = qs[at, :].astype(BF)
            fresh_k = nk32[pl.ds(pl.multiple_of(first, group), group), :].astype(BF)
            fresh_v = nv32[pl.ds(pl.multiple_of(first, group), group), :]
            scores = jnp.zeros((slots, group * heads), F32)
            lengths = jnp.zeros((1, group * heads), jnp.int32)
            for i in range(group):
                own_lanes = lane_row == i
                scores = jnp.where(own_lanes, dot_nt(ck[first + i], q16), scores)
                lengths = jnp.where(own_lanes, len_ref[first + i], lengths)
            scores = jnp.where(position < lengths, scores * score_scale, -jnp.inf)
            own = jnp.sum(jnp.where(own_block, dot_nt(fresh_k, q16), 0.0), axis=0, keepdims=True)
            own = own * score_scale
            highest = jnp.maximum(jnp.max(scores, axis=0, keepdims=True), own)
            e = jnp.exp(scores - highest)
            own_e = jnp.exp(own - highest)
            inv = 1.0 / (jnp.sum(e, axis=0, keepdims=True) + own_e)
            probs = jnp.transpose(e * inv).astype(BF)
            own_p = (own_e * inv).astype(BF).astype(F32)
            own_p = jnp.sum(
                jnp.transpose(jnp.where(own_block, own_p, 0.0)), axis=1, keepdims=True
            )
            o = []
            for i in range(group):
                rows_i = slice(i * heads, (i + 1) * heads)
                old = jnp.dot(probs[rows_i], cv[first + i], preferred_element_type=F32)
                o.append(old + own_p[rows_i] * fresh_v[i : i + 1])
            ao[at, :] = jnp.concatenate(o, axis=0)
            return carry

        lax.fori_loop(0, half_rows // group, some_rows, 0)
        for j in range(heads):
            att[z, h * half_rows : (h + 1) * half_rows, j * HEAD_DIM : (j + 1) * HEAD_DIM] = ao[
                pl.ds(h * half_rows * heads + j, half_rows, stride=heads), :
            ].astype(BF)
        if h == 0:
            pl.semaphore_wait(barrier, 2 * (N - 1))
        piece = att.at[z, pl.ds(h * half_rows, half_rows)]
        send(piece, piece, a_s.at[0, h], a_r.at[z, h], {"ep": z + 1}, z < N - 1)
        send(piece, piece, a_s.at[1, h], a_r.at[z, h], {"ep": z - 1}, z > 0)
        if h == 0:
            load_g = load(5, g_hbm, gw)
            load_u = load(6, u_hbm, uw)
            load_d = load(7, d_hbm, dw)
            send(res_ref, res_all.at[z], res_s.at[0], res_r.at[z], {"ep": t}, z != t)
            for k in range(1, N):
                send(w_all.at[z], w_all.at[z], w_s.at[k], w_r.at[z], {"ep": lax.rem(z + k, N)})
    load_wo.wait()

    my_gain = gain32[:, pl.ds(pl.multiple_of(z * width + t * quarter, quarter), quarter)]

    def piece_of(block, zb, p):
        if p == 0:
            return block.at[pl.ds(pl.multiple_of(jnp.where(zb <= 1, 0, rows), rows), 3 * rows)]
        return block.at[pl.ds(pl.multiple_of(jnp.where(zb <= 1, 3 * rows, 0), rows), rows)]

    def project_rows(i):
        s = order[i]
        if i > 0:
            onward = jnp.where(s < z, z + 1, z - 1)
            go = jnp.logical_and(onward >= 0, onward < N)
            for h in range(2):
                piece = att.at[s, pl.ds(h * half_rows, half_rows)]
                arrived(piece, a_f.at[i, h], a_r.at[s, h])
                send(piece, piece, a_f.at[i, h], a_r.at[s, h], {"ep": onward}, go)

        def project(n, carry):
            cols = pl.ds(pl.multiple_of(n * quarter, quarter), quarter)
            part[i, n] = jnp.dot(att[s], wo[:, cols], preferred_element_type=F32)
            return carry

        lax.fori_loop(0, N, project, 0)

        @pl.when(t == z)
        def _():
            if i > 0:
                arrived(res_all.at[s], res_s.at[0], res_r.at[s])
                src = res_all.at[s]
            else:
                src = res_ref
            for n in range(N):
                part[i, n] = part[i, n] + src[:, n * quarter : (n + 1) * quarter].astype(F32)

        c1s[i] = part[i].astype(BF)
        for k in range(1, N):
            to = lax.rem(t + k, N)
            send(c1s.at[i, to], c1r.at[i, k - 1], c1_s.at[i, k], c1_rs.at[i, k], {"tp": to})

    def sum_rows(i):
        s = order[i]
        total = part[i, t]
        for k in range(1, N):
            arrived(c1r.at[i, k - 1], c1_s.at[i, k], c1_rs.at[i, k])
            total = total + c1r[i, k - 1].astype(F32)
        hg[z, t, pl.ds(pl.multiple_of(s * rows, rows), rows), :] = (total * my_gain).astype(BF)

    def own_side(d, p):
        s = order[d]
        mine = piece_of(hg.at[s, t], s, p)
        if d > 0:
            arrived(mine, cz_s.at[d, p], cz_r.at[s, p])
        send(mine, mine, cx_s.at[d, p], cx_r.at[d, p], {"tp": t_x})
        if d == 0:
            for k in reversed(range(1, N)):
                send(mine, mine, cz_s.at[k, p], cz_r.at[z, p], {"ep": order[k]})
        send(mine, mine, cc_s.at[d, p], cc_r.at[d, p], {"tp": t_core})

    def other_side(d, p):
        s = order[d]
        theirs = piece_of(hg.at[s, t_x], s, p)
        arrived(theirs, cx_s.at[d, p], cx_r.at[d, p])
        send(theirs, theirs, cc_s.at[N + d, p], cc_r.at[N + d, p], {"tp": t_core})

    def gate_up_of(d):
        s = order[d]
        for p in range(2):
            arrived(piece_of(hg.at[s, t_core], s, p), cc_s.at[d, p], cc_r.at[d, p])
            arrived(piece_of(hg.at[s, t_diag], s, p), cc_s.at[N + d, p], cc_r.at[N + d, p])

        def gate_up(b, carry):
            cols = pl.ds(pl.multiple_of(s * width + b * quarter, quarter), quarter)
            block = hg[s, b]
            ga[...] += dot_nt(gw[:, cols], block)
            ua[...] += dot_nt(uw[:, cols], block)
            plain = block.astype(F32) * rgain[:, cols]
            square = plain * plain
            for m in range(quarter // 128):
                ss[...] += square[:, m * 128 : (m + 1) * 128]
            return carry

        lax.fori_loop(0, N, gate_up, 0)

    project_rows(0)
    project_rows(1)
    sum_rows(0)
    project_rows(2)
    sum_rows(1)
    sum_rows(2)
    own_side(0, 0)
    project_rows(3)
    own_side(1, 0)
    sum_rows(3)
    own_side(0, 1)
    other_side(0, 0)
    own_side(2, 0)
    other_side(1, 0)
    own_side(3, 0)
    other_side(0, 1)
    load_g.wait()
    load_u.wait()
    own_side(1, 1)
    other_side(2, 0)
    own_side(2, 1)
    own_side(3, 1)
    gate_up_of(0)
    other_side(3, 0)
    other_side(1, 1)
    gate_up_of(1)
    other_side(2, 1)
    other_side(3, 1)
    gate_up_of(2)
    gate_up_of(3)

    units = ga.shape[0]
    per_expert = units // 2
    dense = w_all[z]
    for i in range(1, N):
        s = order[i]
        arrived(w_all.at[s], w_s.at[i], w_r.at[s])
        dense = dense + w_all[s]
    wsum[...] = dense
    mean_square = jnp.sum(jnp.transpose(ss[...]), axis=0, keepdims=True) * (1.0 / (N * width))
    scale = lax.rsqrt(mean_square + 1e-06)
    for m in range(2):
        at = slice(m * per_expert, (m + 1) * per_expert)
        gate = ga[at] * scale
        up = ua[at] * (scale * wsum[pl.ds(2 * z + m, 1), :])
        ga[at] = gate / (1.0 + jnp.exp(-gate)) * up
    for m in range(units // 128):
        at = slice(m * 128, (m + 1) * 128)
        act[:, at] = jnp.transpose(ga[at]).astype(BF)

    load_d.wait()
    for j, target in enumerate((t_diag, t_x, t_core, t)):

        def down(n, carry):
            cols = pl.ds(pl.multiple_of(target * width + n * quarter, quarter), quarter)
            to = pl.ds(pl.multiple_of(n * quarter, quarter), quarter)
            y = jnp.dot(act[...], dw[:, cols], preferred_element_type=F32)
            if j == 1:
                p1[:, to] = y
            elif j == 3:
                p3[:, to] = y
            else:
                ecs[j // 2, :, to] = y.astype(BF)
            return carry

        lax.fori_loop(0, N, down, 0)
        if j % 2 == 0:
            m = j // 2
            send(ecs.at[m], ecr.at[m], ec_s.at[m], ec_r.at[m], {"tp": t_core})
        if j == 1:
            arrived(ecr.at[0], ec_s.at[0], ec_r.at[0])
            for i in reversed(range(N)):
                s = order[i]
                at = pl.ds(pl.multiple_of(s * rows, rows), rows)
                xs[i] = (p1[at, :] + ecr[0, at, :].astype(F32)).astype(BF)
                send(xs.at[i], xr.at[i], ex_s.at[i], ex_r.at[i], {"tp": t_x})
    arrived(ecr.at[1], ec_s.at[1], ec_r.at[1])
    for i in reversed(range(N)):
        s = order[i]
        at = pl.ds(pl.multiple_of(s * rows, rows), rows)
        y = p3[at, :] + ecr[1, at, :].astype(F32)
        arrived(xr.at[i], ex_s.at[i], ex_r.at[i])
        y = y + xr[i].astype(F32)
        if i > 0:
            zs[i] = y.astype(BF)
            send(zs.at[i], zr.at[z], ez_s.at[i], ez_r.at[z], {"ep": s})
        else:
            for b in range(N):
                cols = pl.ds(pl.multiple_of(t * width + b * quarter, quarter), quarter)
                p1[:rows, b * quarter : (b + 1) * quarter] = (
                    y[:, b * quarter : (b + 1) * quarter]
                    + hg[t, b, pl.ds(pl.multiple_of(z * rows, rows), rows), :].astype(F32)
                    * rgain[:, cols]
                )
    total = p1[:rows, :]
    for i in range(1, N):
        s = order[i]
        arrived(zr.at[s], ez_s.at[i], ez_r.at[s])
        total = total + zr[s].astype(F32)
    out_ref[...] = total.astype(out_ref.dtype)

    for copy, cond in sends:
        if cond is None:
            copy.wait_send()
        else:
            pl.when(cond)(lambda copy=copy: copy.wait_send())


def dense_device(
    queries, cached_key_table, cached_value_table, fresh_token_keys, fresh_token_values, cache_len,
    out_proj, residual, norm_gain, routes, gate_weights, gate_proj, up_proj, down_proj,
):
    rows, heads = queries.shape[0], queries.shape[1] // HEAD_DIM
    width = residual.shape[1]
    quarter = width // N
    units = gate_proj.shape[0] * gate_proj.shape[1]
    all_width = N * width
    all_rows = N * rows
    flat = lambda w: w.reshape(units, all_width)
    vm, hbm = pl.BlockSpec(memory_space=pltpu.VMEM), pl.BlockSpec(memory_space=pltpu.HBM)
    V = pltpu.VMEM
    dma = pltpu.SemaphoreType.DMA
    gain = norm_gain.reshape(-1, 128)
    scratch = [
        pltpu.SMEM(cache_len.shape, jnp.int32), V(queries.shape, BF),
        V(fresh_token_keys.shape, BF), V(fresh_token_values.shape, BF), V(residual.shape, BF),
        V(gain.shape, BF), V((TOP, rows), jnp.int32), V((TOP, rows), F32),
        V(cached_key_table.shape, BF), V(cached_value_table.shape, BF), V(out_proj.shape, BF),
        V((units, all_width), BF), V((units, all_width), BF), V((units, all_width), BF),
        V((rows * heads, HEAD_DIM), F32), V((rows * heads, HEAD_DIM), F32),
        V((rows, HEAD_DIM), F32), V((rows, HEAD_DIM), F32),
        V((1, all_width), F32), V((1, all_width), F32),
        V((N, rows, heads * HEAD_DIM), BF), V((N, rows, width), BF), V((N, TOP, all_rows), F32),
        V((N, N, rows, quarter), F32), V((N, N, rows, quarter), BF), V((N, N - 1, rows, quarter), BF),
        V((N, N, all_rows, quarter), BF), V((units, all_rows), F32), V((units, all_rows), F32),
        V((all_rows, 128), F32), V((all_rows, units), BF),
        V((2, all_rows, width), BF), V((2, all_rows, width), BF),
        V((all_rows, width), F32), V((all_rows, width), F32),
        V((N, rows, width), BF), V((N, rows, width), BF), V((N, rows, width), BF), V((N, rows, width), BF),
        V((TOP, all_rows), F32),
        dma((16,)), dma((1,)), dma((N,)), dma((N,)), dma((N,)),
        dma((2, 2)), dma((N, 2)), dma((N, 2)), dma((N, N)), dma((N, N)),
        dma((N, 2)), dma((N, 2)), dma((N, 2)), dma((N, 2)), dma((2 * N, 2)), dma((2 * N, 2)),
        dma((2,)), dma((2,)), dma((N,)), dma((N,)), dma((N,)), dma((N,)),
    ]
    return pl.pallas_call(
        layer_kernel,
        out_shape=jax.ShapeDtypeStruct((rows, width), BF),
        in_specs=[hbm] * 14,
        out_specs=vm,
        scratch_shapes=scratch,
        compiler_params=pltpu.CompilerParams(
            collective_id=0, has_side_effects=True, vmem_limit_bytes=63 * 1024 * 1024
        ),
        name="layer",
    )(
        cache_len, queries, cached_key_table, cached_value_table, fresh_token_keys,
        fresh_token_values, out_proj, residual, gain, routes.T, gate_weights.T,
        flat(gate_proj), flat(up_proj), flat(down_proj),
    )


def pick_plan(mesh):
    def plan(*args):
        expert_count = args[11].shape[0] * mesh.shape["ep"]
        square = mesh.shape["ep"] == N and mesh.shape["tp"] == N
        one_kv_head = args[1].shape[2] == HEAD_DIM
        if square and one_kv_head and expert_count == TOP:
            return dense_device(*args)
        return per_device(*args)

    return plan


def solution(mesh):
    return jax.shard_map(
        pick_plan(mesh),
        mesh=mesh,
        in_specs=(
            P(("groups", "ep"), "tp"),
            P(("groups", "ep"), None, "tp"),
            P(("groups", "ep"), None, "tp"),
            P(("groups", "ep"), "tp"),
            P(("groups", "ep"), "tp"),
            P(("groups", "ep")),
            P("tp", "ep"),
            P(("groups", "ep"), "tp"),
            P(),
            P(("groups", "ep"), None),
            P(("groups", "ep"), None),
            P("ep", "tp", None),
            P("ep", "tp", None),
            P("ep", "tp", None),
        ),
        out_specs=P(("groups", "ep"), "tp"),
        check_vma=False,
    )
```

```python
import math

import jax
import jax.numpy as jnp
from jax import lax
from jax.experimental import pallas as pl
from jax.experimental.pallas import tpu as pltpu
from jax.sharding import PartitionSpec as P

HEAD_DIM = 128
TOP = 8


def attend_local(
    queries, cached_key_table, cached_value_table, fresh_token_keys, fresh_token_values, cache_len
):
    rows_here = queries.shape[0]
    kv_heads = cached_key_table.shape[2] // HEAD_DIM
    query_group_width = queries.shape[1] // HEAD_DIM // kv_heads
    cache_size = cached_key_table.shape[1]
    query_block = queries.reshape(rows_here, kv_heads, query_group_width, HEAD_DIM)
    key_block = cached_key_table.reshape(rows_here, cache_size, kv_heads, HEAD_DIM)
    value_block = cached_value_table.reshape(rows_here, cache_size, kv_heads, HEAD_DIM)
    newkey_block = fresh_token_keys.reshape(rows_here, kv_heads, HEAD_DIM)
    newval_block = fresh_token_values.reshape(rows_here, kv_heads, HEAD_DIM)
    score_scale = 1.0 / math.sqrt(HEAD_DIM)
    scores = (
        jnp.einsum("rkgd,rjkd->rkgj", query_block, key_block, preferred_element_type=jnp.float32)
        * score_scale
    )
    own_score = (
        jnp.einsum("rkgd,rkd->rkg", query_block, newkey_block, preferred_element_type=jnp.float32)
        * score_scale
    )
    usable = jnp.arange(cache_size, dtype=jnp.int32)[None, :] < cache_len[:, None]
    scores = jnp.where(usable[:, None, None, :], scores, -jnp.inf)
    highest = jnp.maximum(jnp.max(scores, axis=-1), own_score)
    exp_scores = jnp.exp(scores - highest[..., None])
    own_exp = jnp.exp(own_score - highest)
    denominator = jnp.sum(exp_scores, axis=-1) + own_exp
    attn_probs = (exp_scores / denominator[..., None]).astype(jnp.bfloat16)
    own_prob = (own_exp / denominator).astype(jnp.bfloat16)
    attended = jnp.einsum(
        "rkgj,rjkd->rkgd", attn_probs, value_block, preferred_element_type=jnp.float32
    )
    attended = (
        attended
        + own_prob.astype(jnp.float32)[..., None] * newval_block.astype(jnp.float32)[:, :, None, :]
    )
    return attended.reshape(rows_here, -1).astype(jnp.bfloat16)


def per_device(
    queries,
    cached_key_table,
    cached_value_table,
    fresh_token_keys,
    fresh_token_values,
    cache_len,
    out_proj,
    residual,
    norm_gain,
    routes,
    gate_weights,
    gate_proj,
    up_proj,
    down_proj,
):
    attended = attend_local(
        queries,
        cached_key_table,
        cached_value_table,
        fresh_token_keys,
        fresh_token_values,
        cache_len,
    )
    partial_all = jnp.dot(
        lax.all_gather(attended, "ep", axis=0, tiled=True),
        out_proj,
        preferred_element_type=jnp.float32,
    )
    partial_rows = lax.all_to_all(partial_all, "ep", split_axis=0, concat_axis=1, tiled=True)
    ep_count = lax.axis_size("ep")
    tp_index = lax.axis_index("tp")
    rows_here = residual.shape[0]
    col_width = residual.shape[1]
    local_experts = gate_proj.shape[0]
    expert_count = local_experts * ep_count
    capacity = min(rows_here, 2 * rows_here * TOP // expert_count)
    flat_routes = routes.reshape(-1)
    pair_count = flat_routes.shape[0]
    member = (flat_routes[:, None] == jnp.arange(expert_count, dtype=jnp.int32)[None, :]).astype(
        jnp.int32
    )
    earlier = jnp.cumsum(member, axis=0) - member
    position = jnp.sum(earlier * member, axis=1)
    target = flat_routes * capacity + position
    slot_match = (
        jnp.arange(expert_count * capacity, dtype=jnp.int32)[:, None] == target[None, :]
    ).astype(jnp.int32)
    occupied = jnp.sum(slot_match, axis=1)
    source_row = jnp.sum(
        slot_match * (jnp.arange(pair_count, dtype=jnp.int32) // TOP)[None, :], axis=1
    )
    gain_full = norm_gain.astype(jnp.float32)
    own_cols = lax.dynamic_slice_in_dim(
        partial_rows, tp_index * col_width, col_width, 1
    ) + residual.astype(jnp.float32)
    with_residual = lax.dynamic_update_slice_in_dim(partial_rows, own_cols, tp_index * col_width, 1)
    hidden_full = lax.psum(with_residual, "tp")
    mean_square = jnp.mean(hidden_full * hidden_full, axis=-1, keepdims=True)
    normed = (hidden_full * lax.rsqrt(mean_square + 1e-06) * gain_full).astype(jnp.bfloat16)
    hidden = lax.dynamic_slice_in_dim(hidden_full, tp_index * col_width, col_width, 1)
    picked = jnp.where(occupied[:, None] > 0, normed[source_row], jnp.zeros((), normed.dtype))
    arrived = lax.all_to_all(
        picked.reshape(ep_count, local_experts, capacity, normed.shape[1]),
        "ep",
        split_axis=0,
        concat_axis=0,
        tiled=True,
    )
    gate_part = jnp.einsum("aesd,efd->aesf", arrived, gate_proj, preferred_element_type=jnp.float32)
    up_part = jnp.einsum("aesd,efd->aesf", arrived, up_proj, preferred_element_type=jnp.float32)
    activated = (jax.nn.silu(gate_part) * up_part).astype(jnp.bfloat16)
    partial_out = jnp.einsum(
        "aesf,efd->aesd", activated, down_proj, preferred_element_type=jnp.float32
    )
    reduced = lax.psum_scatter(
        partial_out.astype(jnp.bfloat16), "tp", scatter_dimension=3, tiled=True
    ).astype(jnp.float32)
    returned = lax.all_to_all(
        reduced.astype(jnp.bfloat16), "ep", split_axis=0, concat_axis=0, tiled=True
    ).astype(reduced.dtype)
    flat_back = returned.reshape(expert_count * capacity, col_width)
    pair_out = flat_back[target].reshape(rows_here, TOP, col_width)
    mixture = jnp.sum(gate_weights[:, :, None] * pair_out, axis=1)
    return (hidden + mixture).astype(jnp.bfloat16)


MESH = pl.DeviceIdType.MESH
N = 4
BF = jnp.bfloat16
F32 = jnp.float32


def dot_nt(a, b):
    return lax.dot_general(a, b, (((1,), (1,)), ((), ())), preferred_element_type=F32)


def layer_kernel(
    len_hbm, q_hbm, ck_hbm, cv_hbm, nk_hbm, nv_hbm, wo_hbm, res_hbm, gain_hbm, routes_hbm, gw_hbm,
    g_hbm, u_hbm, d_hbm, out_ref,
    len_ref, q_ref, nk_ref, nv_ref, res_ref, gain_ref, routes_ref, gw_ref, ck, cv, wo, gw, uw, dw, qs, ao, nk32, nv32, gain32, rgain, att, res_all, w_all,
    part, c1s, c1r, hg, ga, ua, ss, act, ecs, ecr, p1, p3, xs, xr, zs, zr, wsum,
    load_sem, res_s, res_r, w_s, w_r, a_s, a_f, a_r, c1_s, c1_rs, cz_s, cz_r, cx_s, cx_r,
    cc_s, cc_r, ec_s, ec_r, ex_s, ex_r, ez_s, ez_r,
):
    rows, heads = q_ref.shape[0], q_ref.shape[1] // HEAD_DIM
    slots = ck.shape[1]
    width = res_ref.shape[1]
    quarter = width // N
    half_rows = rows // 2
    z = lax.axis_index("ep")
    t = lax.axis_index("tp")
    core, xpos = lax.rem(t, 2), t // 2
    t_core = 2 * xpos + (1 - core)
    t_x = 2 * (1 - xpos) + core
    t_diag = 2 * (1 - xpos) + (1 - core)
    order = [
        z,
        jnp.where(z == 0, 1, z - 1),
        jnp.where(z == 0, 2, jnp.where(z == N - 1, 1, z + 1)),
        jnp.where(z <= 1, 3, 0),
    ]
    always = z >= 0
    sends = []

    def load(i, src, dst):
        copy = pltpu.make_async_copy(src, dst, load_sem.at[i])
        copy.start()
        return copy

    def send(src, dst, s_sem, r_sem, where, cond=None):
        copy = pltpu.make_async_remote_copy(
            src_ref=src, dst_ref=dst, send_sem=s_sem, recv_sem=r_sem, device_id=where,
            device_id_type=MESH,
        )
        if cond is None:
            copy.start()
        else:
            pl.when(cond)(lambda: copy.start())
        sends.append((copy, cond))

    def arrived(dst, s_sem, r_sem):
        pltpu.make_async_remote_copy(
            src_ref=dst, dst_ref=dst, send_sem=s_sem, recv_sem=r_sem, device_id={"ep": z},
            device_id_type=MESH,
        ).wait_recv()

    load_q = load(8, q_hbm, q_ref)
    loads = []
    for h in range(2):
        piece = pl.ds(h * half_rows, half_rows)
        loads.append(load(2 * h, ck_hbm.at[piece], ck.at[piece]))
        loads.append(load(2 * h + 1, cv_hbm.at[piece], cv.at[piece]))
    pairs = (
        (len_hbm, len_ref), (nk_hbm, nk_ref), (nv_hbm, nv_ref), (res_hbm, res_ref),
        (gain_hbm, gain_ref), (routes_hbm, routes_ref), (gw_hbm, gw_ref),
    )
    small = [load(9 + i, src, dst) for i, (src, dst) in enumerate(pairs)]

    barrier = pltpu.get_barrier_semaphore()
    for k in range(1, N):
        pl.semaphore_signal(barrier, inc=1, device_id={"ep": lax.rem(z + k, N)}, device_id_type=MESH)
        pl.semaphore_signal(barrier, inc=1, device_id={"tp": lax.rem(t + k, N)}, device_id_type=MESH)

    ga[...] = jnp.zeros_like(ga)
    ua[...] = jnp.zeros_like(ua)
    ss[...] = jnp.zeros_like(ss)
    for copy in small:
        copy.wait()
    expert = lax.broadcasted_iota(jnp.int32, (TOP, rows), 0)
    dense = jnp.zeros((TOP, rows), F32)
    for k in range(TOP):
        dense = dense + jnp.where(expert == routes_ref[k : k + 1, :], gw_ref[k : k + 1, :], 0.0)
    owner = lax.broadcasted_iota(jnp.int32, (TOP, N * rows), 1) // rows
    dense = jnp.where(owner == z, jnp.concatenate([dense] * N, axis=1), 0.0)
    w_all[z] = dense
    load_q.wait()
    for h in range(heads):
        qs[pl.ds(h, rows, stride=heads), :] = q_ref[:, h * HEAD_DIM : (h + 1) * HEAD_DIM].astype(F32)
    nk32[...] = nk_ref[...].astype(F32)
    nv32[...] = nv_ref[...].astype(F32)
    gain = gain_ref[...].astype(F32)
    for j in range(gain.shape[0]):
        gain32[:, j * 128 : (j + 1) * 128] = gain[j : j + 1, :]
    rgain[...] = 1.0 / gain32[...]

    score_scale = 1.0 / math.sqrt(HEAD_DIM)
    group = 8
    position = lax.broadcasted_iota(jnp.int32, (slots, group * heads), 0)
    lane_row = lax.broadcasted_iota(jnp.int32, (1, group * heads), 1) // heads
    own_block = lax.broadcasted_iota(jnp.int32, (group, group * heads), 0) == lane_row
    for h in range(2):
        loads[2 * h].wait()
        loads[2 * h + 1].wait()
        if h == 0:
            load_wo = load(4, wo_hbm, wo)

        def some_rows(g, carry):
            first = h * half_rows + g * group
            at = pl.ds(pl.multiple_of(first * heads, group * heads), group * heads)
            q16 = qs[at, :].astype(BF)
            fresh_k = nk32[pl.ds(pl.multiple_of(first, group), group), :].astype(BF)
            fresh_v = nv32[pl.ds(pl.multiple_of(first, group), group), :]
            scores = jnp.zeros((slots, group * heads), F32)
            lengths = jnp.zeros((1, group * heads), jnp.int32)
            for i in range(group):
                own_lanes = lane_row == i
                scores = jnp.where(own_lanes, dot_nt(ck[first + i], q16), scores)
                lengths = jnp.where(own_lanes, len_ref[first + i], lengths)
            scores = jnp.where(position < lengths, scores * score_scale, -jnp.inf)
            own = jnp.sum(jnp.where(own_block, dot_nt(fresh_k, q16), 0.0), axis=0, keepdims=True)
            own = own * score_scale
            highest = jnp.maximum(jnp.max(scores, axis=0, keepdims=True), own)
            e = jnp.exp(scores - highest)
            own_e = jnp.exp(own - highest)
            inv = 1.0 / (jnp.sum(e, axis=0, keepdims=True) + own_e)
            probs = jnp.transpose(e * inv).astype(BF)
            own_p = (own_e * inv).astype(BF).astype(F32)
            own_p = jnp.sum(
                jnp.transpose(jnp.where(own_block, own_p, 0.0)), axis=1, keepdims=True
            )
            o = []
            for i in range(group):
                rows_i = slice(i * heads, (i + 1) * heads)
                old = jnp.dot(probs[rows_i], cv[first + i], preferred_element_type=F32)
                o.append(old + own_p[rows_i] * fresh_v[i : i + 1])
            ao[at, :] = jnp.concatenate(o, axis=0)
            return carry

        lax.fori_loop(0, half_rows // group, some_rows, 0)
        for j in range(heads):
            att[z, h * half_rows : (h + 1) * half_rows, j * HEAD_DIM : (j + 1) * HEAD_DIM] = ao[
                pl.ds(h * half_rows * heads + j, half_rows, stride=heads), :
            ].astype(BF)
        if h == 0:
            pl.semaphore_wait(barrier, 2 * (N - 1))
        piece = att.at[z, pl.ds(h * half_rows, half_rows)]
        send(piece, piece, a_s.at[0, h], a_r.at[z, h], {"ep": z + 1}, z < N - 1)
        send(piece, piece, a_s.at[1, h], a_r.at[z, h], {"ep": z - 1}, z > 0)
        if h == 0:
            load_g = load(5, g_hbm, gw)
            load_u = load(6, u_hbm, uw)
            load_d = load(7, d_hbm, dw)
            send(res_ref, res_all.at[z], res_s.at[0], res_r.at[z], {"ep": t}, z != t)
            for k in range(1, N):
                send(w_all.at[z], w_all.at[z], w_s.at[k], w_r.at[z], {"ep": lax.rem(z + k, N)})
    load_wo.wait()

    my_gain = gain32[:, pl.ds(pl.multiple_of(z * width + t * quarter, quarter), quarter)]

    def piece_of(block, zb, p):
        if p == 0:
            return block.at[pl.ds(pl.multiple_of(jnp.where(zb <= 1, 0, rows), rows), 3 * rows)]
        return block.at[pl.ds(pl.multiple_of(jnp.where(zb <= 1, 3 * rows, 0), rows), rows)]

    def fetch(i):
        s = order[i]
        if i > 0:
            onward = jnp.where(s < z, z + 1, z - 1)
            go = jnp.logical_and(onward >= 0, onward < N)
            for h in range(2):
                piece = att.at[s, pl.ds(h * half_rows, half_rows)]
                arrived(piece, a_f.at[i, h], a_r.at[s, h])
                send(piece, piece, a_f.at[i, h], a_r.at[s, h], {"ep": onward}, go)

    def project_rows(i):
        s = order[i]

        def project(n, carry):
            cols = pl.ds(pl.multiple_of(n * quarter, quarter), quarter)
            part[i, n] = jnp.dot(att[s], wo[:, cols], preferred_element_type=F32)
            return carry

        lax.fori_loop(0, N, project, 0)

        @pl.when(t == z)
        def _():
            if i > 0:
                arrived(res_all.at[s], res_s.at[0], res_r.at[s])
                src = res_all.at[s]
            else:
                src = res_ref
            for n in range(N):
                part[i, n] = part[i, n] + src[:, n * quarter : (n + 1) * quarter].astype(F32)

        c1s[i] = part[i].astype(BF)
        for k in range(1, N):
            to = lax.rem(t + k, N)
            send(c1s.at[i, to], c1r.at[i, k - 1], c1_s.at[i, k], c1_rs.at[i, k], {"tp": to})

    def sum_rows(i):
        s = order[i]
        total = part[i, t]
        for k in range(1, N):
            arrived(c1r.at[i, k - 1], c1_s.at[i, k], c1_rs.at[i, k])
            total = total + c1r[i, k - 1].astype(F32)
        hg[z, t, pl.ds(pl.multiple_of(s * rows, rows), rows), :] = (total * my_gain).astype(BF)

    def own_side(d, p):
        s = order[d]
        mine = piece_of(hg.at[s, t], s, p)
        if d > 0:
            arrived(mine, cz_s.at[d, p], cz_r.at[s, p])
        send(mine, mine, cx_s.at[d, p], cx_r.at[d, p], {"tp": t_x})
        if d == 0:
            for k in reversed(range(1, N)):
                send(mine, mine, cz_s.at[k, p], cz_r.at[z, p], {"ep": order[k]})
        send(mine, mine, cc_s.at[d, p], cc_r.at[d, p], {"tp": t_core})

    def other_side(d, p):
        s = order[d]
        theirs = piece_of(hg.at[s, t_x], s, p)
        arrived(theirs, cx_s.at[d, p], cx_r.at[d, p])
        send(theirs, theirs, cc_s.at[N + d, p], cc_r.at[N + d, p], {"tp": t_core})

    def gate_up_of(d):
        s = order[d]
        for p in range(2):
            arrived(piece_of(hg.at[s, t_core], s, p), cc_s.at[d, p], cc_r.at[d, p])
            arrived(piece_of(hg.at[s, t_diag], s, p), cc_s.at[N + d, p], cc_r.at[N + d, p])

        def gate_up(b, carry):
            cols = pl.ds(pl.multiple_of(s * width + b * quarter, quarter), quarter)
            block = hg[s, b]
            ga[...] += dot_nt(gw[:, cols], block)
            ua[...] += dot_nt(uw[:, cols], block)
            plain = block.astype(F32) * rgain[:, cols]
            square = plain * plain
            for m in range(quarter // 128):
                ss[...] += square[:, m * 128 : (m + 1) * 128]
            return carry

        lax.fori_loop(0, N, gate_up, 0)

    project_rows(0)
    fetch(1)
    project_rows(1)
    sum_rows(0)
    fetch(2)
    project_rows(2)
    sum_rows(1)
    fetch(3)
    sum_rows(2)
    own_side(0, 0)
    project_rows(3)
    own_side(1, 0)
    sum_rows(3)
    own_side(0, 1)
    other_side(0, 0)
    own_side(2, 0)
    other_side(1, 0)
    own_side(3, 0)
    other_side(0, 1)
    load_g.wait()
    load_u.wait()
    own_side(1, 1)
    other_side(2, 0)
    own_side(2, 1)
    own_side(3, 1)
    gate_up_of(0)
    other_side(3, 0)
    other_side(1, 1)
    gate_up_of(1)
    other_side(2, 1)
    other_side(3, 1)
    gate_up_of(2)
    gate_up_of(3)

    units = ga.shape[0]
    per_expert = units // 2
    dense = w_all[z]
    for i in range(1, N):
        s = order[i]
        arrived(w_all.at[s], w_s.at[i], w_r.at[s])
        dense = dense + w_all[s]
    wsum[...] = dense
    mean_square = jnp.sum(jnp.transpose(ss[...]), axis=0, keepdims=True) * (1.0 / (N * width))
    scale = lax.rsqrt(mean_square + 1e-06)
    for m in range(2):
        at = slice(m * per_expert, (m + 1) * per_expert)
        gate = ga[at] * scale
        up = ua[at] * (scale * wsum[pl.ds(2 * z + m, 1), :])
        ga[at] = gate / (1.0 + jnp.exp(-gate)) * up
    for m in range(units // 128):
        at = slice(m * 128, (m + 1) * 128)
        act[:, at] = jnp.transpose(ga[at]).astype(BF)

    load_d.wait()
    for j, target in enumerate((t_diag, t_x, t_core, t)):

        def down(n, carry):
            cols = pl.ds(pl.multiple_of(target * width + n * quarter, quarter), quarter)
            to = pl.ds(pl.multiple_of(n * quarter, quarter), quarter)
            y = jnp.dot(act[...], dw[:, cols], preferred_element_type=F32)
            if j == 1:
                p1[:, to] = y
            elif j == 3:
                p3[:, to] = y
            else:
                ecs[j // 2, :, to] = y.astype(BF)
            return carry

        lax.fori_loop(0, N, down, 0)
        if j % 2 == 0:
            m = j // 2
            for i in reversed(range(N)):
                some = pl.ds(pl.multiple_of(order[i] * rows, rows), rows)
                send(
                    ecs.at[m, some], ecr.at[m, some], ec_s.at[m, i], ec_r.at[m, i], {"tp": t_core}
                )
        if j == 1:
            for i in reversed(range(N)):
                s = order[i]
                some = pl.ds(pl.multiple_of(s * rows, rows), rows)
                arrived(ecr.at[0, some], ec_s.at[0, i], ec_r.at[0, i])
                at = pl.ds(pl.multiple_of(s * rows, rows), rows)
                xs[i] = (p1[at, :] + ecr[0, at, :].astype(F32)).astype(BF)
                send(xs.at[i], xr.at[i], ex_s.at[i], ex_r.at[i], {"tp": t_x})
    for i in reversed(range(N)):
        s = order[i]
        at = pl.ds(pl.multiple_of(s * rows, rows), rows)
        arrived(ecr.at[1, at], ec_s.at[1, i], ec_r.at[1, i])
        y = p3[at, :] + ecr[1, at, :].astype(F32)
        arrived(xr.at[i], ex_s.at[i], ex_r.at[i])
        y = y + xr[i].astype(F32)
        if i > 0:
            zs[i] = y.astype(BF)
            send(zs.at[i], zr.at[z], ez_s.at[i], ez_r.at[z], {"ep": s})
        else:
            for b in range(N):
                cols = pl.ds(pl.multiple_of(t * width + b * quarter, quarter), quarter)
                p1[:rows, b * quarter : (b + 1) * quarter] = (
                    y[:, b * quarter : (b + 1) * quarter]
                    + hg[t, b, pl.ds(pl.multiple_of(z * rows, rows), rows), :].astype(F32)
                    * rgain[:, cols]
                )
    total = p1[:rows, :]
    for i in range(1, N):
        s = order[i]
        arrived(zr.at[s], ez_s.at[i], ez_r.at[s])
        total = total + zr[s].astype(F32)
    out_ref[...] = total.astype(out_ref.dtype)

    for copy, cond in sends:
        if cond is None:
            copy.wait_send()
        else:
            pl.when(cond)(lambda copy=copy: copy.wait_send())


def dense_device(
    queries, cached_key_table, cached_value_table, fresh_token_keys, fresh_token_values, cache_len,
    out_proj, residual, norm_gain, routes, gate_weights, gate_proj, up_proj, down_proj,
):
    rows, heads = queries.shape[0], queries.shape[1] // HEAD_DIM
    width = residual.shape[1]
    quarter = width // N
    units = gate_proj.shape[0] * gate_proj.shape[1]
    all_width = N * width
    all_rows = N * rows
    flat = lambda w: w.reshape(units, all_width)
    vm, hbm = pl.BlockSpec(memory_space=pltpu.VMEM), pl.BlockSpec(memory_space=pltpu.HBM)
    V = pltpu.VMEM
    dma = pltpu.SemaphoreType.DMA
    gain = norm_gain.reshape(-1, 128)
    scratch = [
        pltpu.SMEM(cache_len.shape, jnp.int32), V(queries.shape, BF),
        V(fresh_token_keys.shape, BF), V(fresh_token_values.shape, BF), V(residual.shape, BF),
        V(gain.shape, BF), V((TOP, rows), jnp.int32), V((TOP, rows), F32),
        V(cached_key_table.shape, BF), V(cached_value_table.shape, BF), V(out_proj.shape, BF),
        V((units, all_width), BF), V((units, all_width), BF), V((units, all_width), BF),
        V((rows * heads, HEAD_DIM), F32), V((rows * heads, HEAD_DIM), F32),
        V((rows, HEAD_DIM), F32), V((rows, HEAD_DIM), F32),
        V((1, all_width), F32), V((1, all_width), F32),
        V((N, rows, heads * HEAD_DIM), BF), V((N, rows, width), BF), V((N, TOP, all_rows), F32),
        V((N, N, rows, quarter), F32), V((N, N, rows, quarter), BF), V((N, N - 1, rows, quarter), BF),
        V((N, N, all_rows, quarter), BF), V((units, all_rows), F32), V((units, all_rows), F32),
        V((all_rows, 128), F32), V((all_rows, units), BF),
        V((2, all_rows, width), BF), V((2, all_rows, width), BF),
        V((all_rows, width), F32), V((all_rows, width), F32),
        V((N, rows, width), BF), V((N, rows, width), BF), V((N, rows, width), BF), V((N, rows, width), BF),
        V((TOP, all_rows), F32),
        dma((16,)), dma((1,)), dma((N,)), dma((N,)), dma((N,)),
        dma((2, 2)), dma((N, 2)), dma((N, 2)), dma((N, N)), dma((N, N)),
        dma((N, 2)), dma((N, 2)), dma((N, 2)), dma((N, 2)), dma((2 * N, 2)), dma((2 * N, 2)),
        dma((2, N)), dma((2, N)), dma((N,)), dma((N,)), dma((N,)), dma((N,)),
    ]
    return pl.pallas_call(
        layer_kernel,
        out_shape=jax.ShapeDtypeStruct((rows, width), BF),
        in_specs=[hbm] * 14,
        out_specs=vm,
        scratch_shapes=scratch,
        compiler_params=pltpu.CompilerParams(
            collective_id=0, has_side_effects=True, vmem_limit_bytes=63 * 1024 * 1024
        ),
        name="layer",
    )(
        cache_len, queries, cached_key_table, cached_value_table, fresh_token_keys,
        fresh_token_values, out_proj, residual, gain, routes.T, gate_weights.T,
        flat(gate_proj), flat(up_proj), flat(down_proj),
    )


def pick_plan(mesh):
    def plan(*args):
        expert_count = args[11].shape[0] * mesh.shape["ep"]
        square = mesh.shape["ep"] == N and mesh.shape["tp"] == N
        one_kv_head = args[1].shape[2] == HEAD_DIM
        if square and one_kv_head and expert_count == TOP:
            return dense_device(*args)
        return per_device(*args)

    return plan


def solution(mesh):
    return jax.shard_map(
        pick_plan(mesh),
        mesh=mesh,
        in_specs=(
            P(("groups", "ep"), "tp"),
            P(("groups", "ep"), None, "tp"),
            P(("groups", "ep"), None, "tp"),
            P(("groups", "ep"), "tp"),
            P(("groups", "ep"), "tp"),
            P(("groups", "ep")),
            P("tp", "ep"),
            P(("groups", "ep"), "tp"),
            P(),
            P(("groups", "ep"), None),
            P(("groups", "ep"), None),
            P("ep", "tp", None),
            P("ep", "tp", None),
            P("ep", "tp", None),
        ),
        out_specs=P(("groups", "ep"), "tp"),
        check_vma=False,
    )
```
